256 devices in a mesh: batch: 16 (over z, core), tensor: 16 (over y, x).
Axes of the slice: x: 4, y: 4, z: 8, core: 2. Of those that a mesh axis runs over, the one named last changes fastest.
Arguments:
- inputs: bfloat16 [3, 256, 8192], P(None, None, 'batch'), may hold values from -40 to 40
- in_gain: float32 [8192], P('batch'), may hold values from 0.1 to 1.9
- qkv_weight: bfloat16 [8192, 24576], P('batch', 'tensor'), may hold values from -0.0625 to 0.0625
- decay: float32 [64], P('tensor'), may hold values from 0.25 to 0.99
- state: float32 [256, 64, 128, 128], P('batch', 'tensor'), may hold values from -1.8 to 1.8
- head_gain: float32 [8192], P('tensor'), may hold values from 0.1 to 1.9
- out_weight: bfloat16 [8192, 8192], P('tensor', 'batch'), may hold values from -0.0625 to 0.0625
- mid_gain: float32 [8192], P('batch'), may hold values from 0.1 to 1.9
- up_weight: bfloat16 [8192, 28672], P('batch', 'tensor'), may hold values from -0.0625 to 0.0625
- down_weight: bfloat16 [28672, 8192], P('tensor', 'batch'), may hold values from -0.03125 to 0.03125
- att_mask: int32 [3, 256, 8192], P(None, 'batch', 'tensor'), may hold values 0 or 1
- ffn_mask: int32 [3, 256, 28672], P(None, 'batch', 'tensor'), may hold values 0 or 1
Outputs:
- outputs: bfloat16 [3, 256, 8192], P(None, 'tensor', 'batch')
The draws below stay inside these ranges and needn't reach their ends.
All inputs are finite; a program needn't handle non-finite values. No bound on the sum of `att_mask` or of `ffn_mask` on one device may be relied on, other than what follows from the above.
Results may differ from the reference program's by a relative error of at most 0.0038.
Values may be sent and summed in bfloat16 or wider, within the bound.
No kernel may reach another device: no remote copies, remote signals or barrier semaphores. Data moves between devices by JAX's collectives and lax.ppermute only.
A program may use at most 64 MiB of HBM per device.

```python
import math
import jax
import jax.numpy as jnp
from jax import lax

D = 8192
H = 64
DH = 128
FF = 28672
STEPS = 3
REQUESTS = 256


def draw_inputs(key, part):
    key = jax.random.fold_in(key, 7)
    pieces = jax.random.split(key, 4)
    position = jnp.arange(D, dtype=jnp.float32) / (D - 1)
    ramp = jnp.sqrt((1.0 + 2.0 * position) / 2.0)
    rough = jnp.exp(jax.random.uniform(pieces[0], (D,), jnp.float32, -1.15, 1.15))
    base = jnp.clip(jax.random.normal(pieces[1], (STEPS, REQUESTS, D), jnp.float32), -4.0, 4.0)
    rows = jnp.exp(jax.random.uniform(pieces[3], (STEPS, REQUESTS, 1), jnp.float32, -0.7, 0.7))
    return (base * rows * (ramp * rough)).astype(jnp.bfloat16)


def with_ends(drawn, own_key, least, largest):
    dims = drawn.shape
    index_at = [jax.random.randint(jax.random.fold_in(own_key, axis), (), 0, dims[axis]) for axis in range(len(dims))]
    drawn = drawn.at[tuple(index_at)].set(least)
    longest = dims.index(max(dims))
    index_at[longest] = (index_at[longest] + 1) % dims[longest]
    return drawn.at[tuple(index_at)].set(largest)


def block_levels(rng, shape, cuts, low, largest):
    def one(dim, blocks):
        steps = jax.random.uniform(jax.random.fold_in(jax.random.fold_in(rng, 6), dim), (blocks,), jnp.float32, low / len(cuts), largest / len(cuts))
        return jnp.repeat(jnp.exp(steps), shape[dim] // blocks).reshape((-1,) + (1,) * (len(shape) - dim - 1))

    gain = one(*cuts[0])
    for cut in cuts[1:]:
        gain = gain * one(*cut)
    return gain


def gaussian(key, shape, width, most, shards=(), kind=jnp.bfloat16):
    result = jax.random.normal(key, shape, jnp.float32) * width
    if len(shards) > 0:
        result = block_levels(key, shape, shards, -0.22, 0.18) * result
    return jnp.clip(result, min=-most, max=most).astype(kind)


def setup_inputs(seed: int = 0) -> dict:
    streams_of = jax.random.split(jax.random.key(seed), 13)
    return {
        "inputs": draw_inputs(jax.random.fold_in(streams_of[12], 71), 0),
        "in_gain": jnp.clip(1.0 + 0.18 * jax.random.normal(streams_of[1], (D,), jnp.float32), 0.1, 1.9),
        "qkv_weight": gaussian(streams_of[2], (D, H * 3 * DH), D ** -0.5, 0.0625, ((0, 16), (1, 16))),
        "decay": jnp.clip(jnp.exp(math.log(0.99) - 1.37624403 * jax.random.uniform(streams_of[3], (H,), jnp.float32) ** block_levels(streams_of[3], (H,), ((0, 16),), -0.2, 0.2)), 0.25, 0.99),
        "state": gaussian(streams_of[4], (REQUESTS, H, DH, DH), 0.3, 1.8, ((0, 16), (1, 16)), jnp.float32),
        "head_gain": jnp.clip(1.0 + 0.18 * jax.random.normal(streams_of[5], (H * DH,), jnp.float32), 0.1, 1.9),
        "out_weight": gaussian(streams_of[6], (H * DH, D), (H * DH) ** -0.5, 0.0625, ((0, 16), (1, 16))),
        "mid_gain": jnp.clip(1.0 + 0.18 * jax.random.normal(streams_of[7], (D,), jnp.float32), 0.1, 1.9),
        "up_weight": gaussian(streams_of[8], (D, FF), D ** -0.5, 0.0625, ((0, 16), (1, 16))),
        "down_weight": gaussian(streams_of[9], (FF, D), FF ** -0.5, 0.03125, ((0, 16), (1, 16))),
        "att_mask": with_ends((jax.random.randint(streams_of[10], (STEPS, REQUESTS, H * DH), 0, 10) < 3).astype(jnp.int32), jax.random.fold_in(streams_of[10], 1), 0, 1),
        "ffn_mask": with_ends((jax.random.randint(streams_of[11], (STEPS, REQUESTS, FF), 0, 10) < 3).astype(jnp.int32), jax.random.fold_in(streams_of[11], 1), 0, 1),
    }


EPS = 1e-06

def head_chain(items):
    start_state, queries, keys_all, values_all, rate = items
    carried = start_state
    results = []
    for step in range(STEPS):
        carried = rate * carried + jnp.einsum('ri,rj->rij', keys_all[step], values_all[step], precision=lax.Precision.HIGHEST)
        results.append(jnp.einsum('ri,rij->rj', queries[step], carried, precision=lax.Precision.HIGHEST))
    return jnp.stack(results)

def reference(inputs, in_gain, qkv_weight, decay, state, head_gain, out_weight, mid_gain, up_weight, down_weight, att_mask, ffn_mask):
    widened = inputs.astype(jnp.float32)
    scale = DH ** (-0.5)
    projections = []
    for step in range(STEPS):
        current = widened[step]
        inv_one = lax.rsqrt(lax.optimization_barrier(jnp.mean(current * current, axis=-1, keepdims=True)) + EPS)
        normed = (current * in_gain * inv_one).astype(jnp.bfloat16)
        projected = jnp.dot(normed, qkv_weight, preferred_element_type=jnp.float32)
        projections.append(projected.reshape(REQUESTS, H, 3, DH))
    projected = jnp.stack(projections)
    queries = jnp.moveaxis(projected[:, :, :, 0, :] * scale, 2, 0)
    keys_all = jnp.moveaxis(projected[:, :, :, 1, :] * scale, 2, 0)
    values_all = jnp.moveaxis(projected[:, :, :, 2, :], 2, 0)
    attended = lax.map(head_chain, (jnp.moveaxis(state, 1, 0), queries, keys_all, values_all, decay))
    attended = jnp.moveaxis(attended, 0, 2)
    attended = attended * lax.rsqrt(lax.optimization_barrier(jnp.mean(attended * attended, axis=-1, keepdims=True)) + EPS)
    attended = attended.reshape(STEPS, REQUESTS, H * DH)
    results = []
    for step in range(STEPS):
        current = widened[step]
        spiked = (attended[step] * head_gain * att_mask[step]).astype(jnp.bfloat16)
        mixed = current + jnp.dot(spiked, out_weight, preferred_element_type=jnp.float32)
        inv_two = lax.rsqrt(lax.optimization_barrier(jnp.mean(mixed * mixed, axis=-1, keepdims=True)) + EPS)
        hidden_in = (mixed * mid_gain * inv_two).astype(jnp.bfloat16)
        gate_sum = jnp.dot(hidden_in, up_weight, preferred_element_type=jnp.float32)
        fired = (ffn_mask[step] * jax.nn.silu(gate_sum)).astype(jnp.bfloat16)
        final = mixed + jnp.dot(fired, down_weight, preferred_element_type=jnp.float32)
        results.append(final.astype(jnp.bfloat16))
    return jnp.stack(results)
```

```python
import functools

import jax
import jax.numpy as jnp
from jax import lax
from jax.experimental import pallas as pl
from jax.experimental.pallas import tpu as pltpu
from jax.sharding import Mesh
from jax.sharding import PartitionSpec as P

D = 8192
STEPS = 3
DH = 128
EPS = 1e-06
LANES = 128
BATCH = ("z", "core")
TENSOR = ("y", "xh", "xl")
TENSOR_ROWS = ("xl", "y", "xh")


def pieces_of(sums):
    high = lax.reduce_precision(sums, 8, 7)
    middle = lax.reduce_precision(sums - high, 8, 7)
    low = sums - high - middle
    lane = lax.broadcasted_iota(jnp.int32, sums.shape[:-1] + (LANES,), sums.ndim - 1)
    out = jnp.where(lane == 0, high, jnp.where(lane == 1, middle, jnp.where(lane == 2, low, 0.0)))
    return out.astype(jnp.bfloat16)


def swap_cores(value):
    return lax.ppermute(value, "core", [(0, 1), (1, 0)])


def attention_kernel(decay_ref, parts_ref, sums_ref, state_ref, gain_ref, mask_ref, out_ref):
    head = pl.program_id(0)
    rows = parts_ref.shape[1]
    mine = rows // STEPS
    squares = jnp.sum(jnp.sum(sums_ref[...].astype(jnp.float32), axis=0), axis=-1, keepdims=True)
    inverse = lax.rsqrt(squares / D + EPS)
    parts = jnp.sum(parts_ref[...].astype(jnp.float32), axis=0) * inverse
    scale = DH ** (-0.5)
    queries = parts[:, :DH] * scale
    keys = parts[:, DH : 2 * DH] * scale
    values = parts[:, 2 * DH :]
    rate = decay_ref[head]
    turned = queries.T
    found = [[] for _ in range(STEPS)]
    for request in range(mine):
        block = state_ref[request, 0]
        for step in range(STEPS):
            at = step * mine + request
            found[step].append(jnp.sum(turned[:, at : at + 1] * block, axis=0, keepdims=True))
    power = rate
    for step in range(STEPS):
        here = slice(step * mine, (step + 1) * mine)
        total = power * jnp.concatenate(found[step], axis=0)
        power = power * rate
        factor = None
        for earlier in range(step, -1, -1):
            there = slice(earlier * mine, (earlier + 1) * mine)
            score = jnp.sum(queries[here] * keys[there], axis=-1, keepdims=True)
            if factor is not None:
                score = score * factor
            total = total + score * values[there]
            factor = rate if factor is None else factor * rate
        total = total * lax.rsqrt(jnp.mean(total * total, axis=-1, keepdims=True) + EPS)
        spiked = total * gain_ref[...] * mask_ref[step].astype(jnp.float32)
        out_ref[here, :] = spiked.astype(jnp.bfloat16)


def attention(decay, parts, state, head_gain, att_mask):
    sources, rows, width = parts.shape
    mine, heads = state.shape[:2]
    last = width // LANES - 1
    return pl.pallas_call(
        attention_kernel,
        grid=(heads,),
        in_specs=[
            pl.BlockSpec(memory_space=pltpu.SMEM),
            pl.BlockSpec((sources, rows, 3 * DH), lambda h: (0, 0, h)),
            pl.BlockSpec((sources, rows, LANES), lambda h: (0, 0, last)),
            pl.BlockSpec((mine, 1, DH, DH), lambda h: (0, h, 0, 0)),
            pl.BlockSpec((1, DH), lambda h: (0, h)),
            pl.BlockSpec((STEPS, mine, DH), lambda h: (0, 0, h)),
        ],
        out_specs=pl.BlockSpec((rows, DH), lambda h: (0, h)),
        out_shape=jax.ShapeDtypeStruct((rows, heads * DH), jnp.bfloat16),
        compiler_params=pltpu.CompilerParams(vmem_limit_bytes=32 * 1024 * 1024),
    )(decay, parts, parts, state, head_gain[None, :], att_mask)


def sum_to_owner(rows, weight, sums, core):
    cores, zs, each, depth = rows.shape
    width = weight.shape[1]

    def product(which):
        picked = lax.dynamic_index_in_dim(rows, which, 0, keepdims=False).reshape(zs * each, depth)
        return jnp.dot(picked, weight, preferred_element_type=jnp.float32).astype(jnp.bfloat16)

    theirs = swap_cores(product(1 - core))
    their_sums = swap_cores(lax.dynamic_index_in_dim(sums, 1 - core, 0, keepdims=False))
    ours = product(core)
    total = (ours.astype(jnp.float32) + theirs.astype(jnp.float32)).astype(jnp.bfloat16)
    squares = lax.dynamic_index_in_dim(sums, core, 0, keepdims=False) + their_sums
    sent = jnp.concatenate([total.reshape(zs, each, width), pieces_of(squares)], axis=-1)
    return lax.all_to_all(sent, "z", 0, 0, tiled=True)


def gather_rows(value, zs):
    along_z = lax.all_to_all(jnp.broadcast_to(value[None], (zs,) + value.shape), "z", 0, 0, tiled=True)
    both = lax.all_gather(along_z, "core", axis=0, tiled=False)
    return both.reshape(2 * zs * value.shape[0], value.shape[1])


def on_device(
    inputs,
    in_gain,
    qkv_weight,
    decay,
    state,
    head_gain,
    out_weight,
    mid_gain,
    up_weight,
    down_weight,
    att_mask,
    ffn_mask,
):
    cores = lax.axis_size("core")
    zs = lax.axis_size("z")
    core = lax.axis_index("core")
    share = inputs.shape[1] // (zs * cores)
    features = inputs.shape[2]
    each = STEPS * share
    ordered = inputs.reshape(STEPS, zs, cores, share, features).transpose(2, 1, 0, 3, 4)
    current = ordered.reshape(cores, zs, each, features).astype(jnp.float32)
    squares = jnp.sum(current * current, axis=-1, keepdims=True)
    scaled = (current * in_gain).astype(jnp.bfloat16)
    parts = sum_to_owner(scaled, qkv_weight, squares, core)
    spiked = attention(decay, parts, state, head_gain, att_mask)

    everyone = gather_rows(spiked, zs)
    partial = jnp.dot(everyone, out_weight, preferred_element_type=jnp.float32).astype(jnp.bfloat16)
    partial = lax.all_to_all(partial.reshape(cores * zs, each, features), TENSOR_ROWS, 0, 0, tiled=True)
    start = lax.axis_index(TENSOR) * share
    kept = lax.dynamic_slice_in_dim(inputs, start, share, 1).reshape(each, features).astype(jnp.float32)
    mixed = kept + jnp.sum(partial.astype(jnp.float32), axis=0)

    hidden = (mixed * mid_gain).astype(jnp.bfloat16)
    hidden = jnp.broadcast_to(hidden[None], (cores * zs, each, features))
    hidden = lax.all_to_all(hidden, TENSOR_ROWS, 0, 0, tiled=True)
    hidden = hidden.reshape(cores, zs, each, features)
    back = hidden.astype(jnp.float32) * (1.0 / mid_gain)
    squares = jnp.sum(back * back, axis=-1, keepdims=True)
    parts = sum_to_owner(hidden, up_weight, squares, core)
    total = jnp.sum(parts.astype(jnp.float32), axis=0)
    units = up_weight.shape[1]
    inverse = lax.rsqrt(jnp.sum(total[:, units:], axis=-1, keepdims=True) / D + EPS)
    gate = total[:, :units] * inverse
    fired = ffn_mask.reshape(each, units) * (gate / (1.0 + jnp.exp(-gate)))

    everyone = gather_rows(fired.astype(jnp.bfloat16), zs)
    partial = jnp.dot(everyone, down_weight, preferred_element_type=jnp.float32).astype(jnp.bfloat16)
    partial = lax.all_to_all(partial.reshape(cores * zs, each, features), TENSOR_ROWS, 0, 0, tiled=True)
    final = mixed + jnp.sum(partial.astype(jnp.float32), axis=0)
    return final.astype(jnp.bfloat16).reshape(STEPS, share, features)


def solution(mesh):
    devices = mesh.devices.reshape(8, 2, 4, 2, 2)
    inner = Mesh(devices, ("z", "core", "y", "xh", "xl"))
    return jax.shard_map(
        on_device,
        mesh=inner,
        in_specs=(
            P(None, None, BATCH),
            P(BATCH),
            P(BATCH, TENSOR),
            P(TENSOR),
            P(BATCH, TENSOR, None, None),
            P(TENSOR),
            P(TENSOR, BATCH),
            P(BATCH),
            P(BATCH, TENSOR),
            P(TENSOR, BATCH),
            P(None, BATCH, TENSOR),
            P(None, BATCH, TENSOR),
        ),
        out_specs=P(None, TENSOR, BATCH),
        check_vma=False,
    )
```

```python
import functools

import jax
import jax.numpy as jnp
from jax import lax
from jax.experimental import pallas as pl
from jax.experimental.pallas import tpu as pltpu
from jax.sharding import Mesh
from jax.sharding import PartitionSpec as P

D = 8192
STEPS = 3
DH = 128
EPS = 1e-06
LANES = 128
BATCH = ("z", "core")
TENSOR = ("y", "x")
VMEM = pltpu.CompilerParams(vmem_limit_bytes=48 * 1024 * 1024)


def swap_cores(value):
    return lax.ppermute(value, "core", [(0, 1), (1, 0)])


def pass_on(value):
    zs = lax.axis_size("z")
    pairs = []
    for z in range(zs):
        pairs.append((2 * z, 2 * ((z + 1) % zs)))
        pairs.append((2 * z + 1, 2 * ((z - 1) % zs) + 1))
    return lax.ppermute(value, BATCH, pairs)


def pieces_of(sums, source):
    high = lax.reduce_precision(sums, 8, 7)
    middle = lax.reduce_precision(sums - high, 8, 7)
    low = sums - high - middle
    lane = lax.broadcasted_iota(jnp.int32, (sums.shape[0], LANES), 1) - 3 * source
    return jnp.where(lane == 0, high, jnp.where(lane == 1, middle, jnp.where(lane == 2, low, 0.0)))


def product_kernel(chips, first, place_ref, rows_ref, gain_ref, weight_ref, out_ref, picked_ref):
    width = weight_ref.shape[1]
    share = picked_ref.shape[0] // (2 * STEPS * chips)
    zs = rows_ref.shape[1] // (2 * share) if first else rows_ref.shape[0] // 2
    start, source = place_ref[0], place_ref[1]
    for c in range(chips):
        chip = start + c
        chip = jnp.where(chip >= zs, chip - zs, chip)
        for core in range(2):
            for step in range(STEPS):
                at = ((c * 2 + core) * STEPS + step) * share
                if first:
                    from_row = pl.multiple_of(chip * (2 * share) + core * share, share)
                    values = rows_ref[step, pl.ds(from_row, share), :].astype(jnp.float32)
                    picked_ref[at : at + share, :] = (values * gain_ref[...]).astype(jnp.bfloat16)
                else:
                    block = rows_ref[chip * 2 + core, step * share : (step + 1) * share, :]
                    picked_ref[at : at + share, :] = block
                    values = block.astype(jnp.float32) * gain_ref[...]
                squares = jnp.sum(values * values, axis=-1, keepdims=True)
                out_ref[at : at + share, width:] = pieces_of(squares, source).astype(out_ref.dtype)
    chunk = 256
    for at in range(0, width, chunk):
        out_ref[:, at : at + chunk] = jnp.dot(
            picked_ref[...], weight_ref[:, at : at + chunk], preferred_element_type=jnp.float32
        ).astype(out_ref.dtype)


def product(rows, gain, weight, chips, start, source, first, dtype):
    share = (rows.shape[1] // 16) if first else rows.shape[1] // STEPS
    count = chips * 2 * STEPS * share
    depth, width = weight.shape
    place = jnp.stack([start, source]).astype(jnp.int32)
    out = pl.pallas_call(
        functools.partial(product_kernel, chips, first),
        in_specs=[pl.BlockSpec(memory_space=pltpu.SMEM)] + [pl.BlockSpec(memory_space=pltpu.VMEM)] * 3,
        out_specs=pl.BlockSpec(memory_space=pltpu.VMEM),
        out_shape=jax.ShapeDtypeStruct((count, width + LANES), dtype),
        scratch_shapes=[pltpu.VMEM((count, depth), jnp.bfloat16)],
        compiler_params=VMEM,
    )(place, rows, gain[None, :], weight)
    return out.reshape(chips, 2, STEPS * share, width + LANES)


def sum_to_owner(rows, gain, weight, first):
    zs = lax.axis_size("z")
    half = zs // 2
    z, core = lax.axis_index("z"), lax.axis_index("core")
    source = z * 2 + core
    ahead = core == 0
    theirs_from = jnp.where(ahead, z + half, z + 1) % zs
    mine_from = jnp.where(ahead, z, z + half) % zs
    theirs = product(rows, gain, weight, half, theirs_from, source, first, jnp.bfloat16)
    got = swap_cores(theirs)
    mine = product(rows, gain, weight, half + 1, mine_from, source, first, jnp.bfloat16)

    def at(distance):
        in_mine = jnp.where(ahead, distance, half - distance)
        in_got = jnp.where(ahead, distance - 1, half - distance)
        own = lax.dynamic_index_in_dim(mine, in_mine, 0, keepdims=False).astype(jnp.float32)
        other = lax.dynamic_index_in_dim(got, in_got, 0, keepdims=False).astype(jnp.float32)
        return own + other

    carried = lax.dynamic_index_in_dim(at(half), core, 0, keepdims=False).astype(jnp.bfloat16)
    carried = pass_on(carried)
    which = lax.broadcasted_iota(jnp.int32, (2, 1, 1), 0) == core
    total = at(half - 1) + jnp.where(which, carried.astype(jnp.float32)[None], 0.0)
    for distance in range(half - 2, -1, -1):
        carried = pass_on(total.astype(jnp.bfloat16)).astype(jnp.float32)
        if distance > 0:
            total = at(distance) + carried
    own = lax.dynamic_index_in_dim(mine, jnp.where(ahead, 0, half), 0, keepdims=False)
    total = own.astype(jnp.float32) + carried
    away = lax.dynamic_index_in_dim(total, 1 - core, 0, keepdims=False).astype(jnp.bfloat16)
    return lax.dynamic_index_in_dim(total, core, 0, keepdims=False), swap_cores(away)


def attention_kernel(decay_ref, ours_ref, our_sums_ref, theirs_ref, their_sums_ref, state_ref, gain_ref, mask_ref, out_ref):
    head = pl.program_id(0)
    rows = ours_ref.shape[0]
    mine = rows // STEPS
    squares = jnp.sum(our_sums_ref[...] + their_sums_ref[...].astype(jnp.float32), axis=-1, keepdims=True)
    parts = (ours_ref[...] + theirs_ref[...].astype(jnp.float32)) * lax.rsqrt(squares / D + EPS)
    scale = DH ** (-0.5)
    queries = parts[:, :DH] * scale
    keys = parts[:, DH : 2 * DH] * scale
    values = parts[:, 2 * DH :]
    rate = decay_ref[head]
    turned = queries.T
    found = [[] for _ in range(STEPS)]
    for request in range(mine):
        block = state_ref[request, 0]
        for step in range(STEPS):
            at = step * mine + request
            found[step].append(jnp.sum(turned[:, at : at + 1] * block, axis=0, keepdims=True))
    power = rate
    for step in range(STEPS):
        here = slice(step * mine, (step + 1) * mine)
        total = power * jnp.concatenate(found[step], axis=0)
        power = power * rate
        factor = None
        for earlier in range(step, -1, -1):
            there = slice(earlier * mine, (earlier + 1) * mine)
            score = jnp.sum(queries[here] * keys[there], axis=-1, keepdims=True)
            if factor is not None:
                score = score * factor
            total = total + score * values[there]
            factor = rate if factor is None else factor * rate
        total = total * lax.rsqrt(jnp.mean(total * total, axis=-1, keepdims=True) + EPS)
        spiked = total * gain_ref[...] * mask_ref[step].astype(jnp.float32)
        out_ref[here, :] = spiked.astype(jnp.bfloat16)


def attention(decay, ours, theirs, state, head_gain, att_mask):
    rows, width = ours.shape
    mine, heads = state.shape[:2]
    last = width // LANES - 1
    return pl.pallas_call(
        attention_kernel,
        grid=(heads,),
        in_specs=[
            pl.BlockSpec(memory_space=pltpu.SMEM),
            pl.BlockSpec((rows, 3 * DH), lambda h: (0, h)),
            pl.BlockSpec((rows, LANES), lambda h: (0, last)),
            pl.BlockSpec((rows, 3 * DH), lambda h: (0, h)),
            pl.BlockSpec((rows, LANES), lambda h: (0, last)),
            pl.BlockSpec((mine, 1, DH, DH), lambda h: (0, h, 0, 0)),
            pl.BlockSpec((1, DH), lambda h: (0, h)),
            pl.BlockSpec((STEPS, mine, DH), lambda h: (0, 0, h)),
        ],
        out_specs=pl.BlockSpec((rows, DH), lambda h: (0, h)),
        out_shape=jax.ShapeDtypeStruct((rows, heads * DH), jnp.bfloat16),
        compiler_params=VMEM,
    )(decay, ours, ours, theirs, theirs, state, head_gain[None, :], att_mask)


def gathered_product(value, weight):
    zs = lax.axis_size("z")
    half = zs // 2
    z, core = lax.axis_index("z"), lax.axis_index("core")
    towards = jnp.where(core == 0, -1, 1)
    rows, width = value.shape[0], weight.shape[1]
    out = jnp.zeros((zs, 2, rows, width), jnp.bfloat16)

    def multiply(blocks):
        return jnp.dot(blocks.reshape(-1, blocks.shape[-1]), weight, preferred_element_type=jnp.float32).astype(
            jnp.bfloat16
        ).reshape(blocks.shape[:-1] + (width,))

    def put(out, blocks, chip):
        return lax.dynamic_update_slice(out, blocks[None], ((chip + zs) % zs, 0, 0, 0))

    sibling = swap_cores(value)
    low, high = jnp.where(core == 0, value, sibling), jnp.where(core == 0, sibling, value)
    moving = jnp.stack([low, high])
    done = multiply(moving)
    out = put(out, done, z)
    for distance in range(1, half):
        moving = pass_on(moving)
        other = swap_cores(moving)
        done = multiply(jnp.stack([moving, other]))
        out = put(out, done[0], z + towards * distance)
        out = put(out, done[1], z - towards * distance)
    last = pass_on(lax.dynamic_index_in_dim(moving, core, 0, keepdims=False))
    other = swap_cores(last)
    low, high = jnp.where(core == 0, last, other), jnp.where(core == 0, other, last)
    return put(out, multiply(jnp.stack([low, high])), z + half)


def on_device(
    inputs,
    in_gain,
    qkv_weight,
    decay,
    state,
    head_gain,
    out_weight,
    mid_gain,
    up_weight,
    down_weight,
    att_mask,
    ffn_mask,
):
    blocks = lax.axis_size("core") * lax.axis_size("z")
    share = inputs.shape[1] // blocks
    features = inputs.shape[2]
    each = STEPS * share
    ours, theirs = sum_to_owner(inputs, in_gain, qkv_weight, True)
    spiked = attention(decay, ours, theirs, state, head_gain, att_mask)

    everyone = lax.all_gather(spiked, BATCH, axis=0, tiled=True)
    partial = jnp.dot(everyone, out_weight, preferred_element_type=jnp.float32).astype(jnp.bfloat16)
    partial = lax.all_to_all(partial.reshape(blocks, each, features), TENSOR, 0, 0, tiled=True)
    start = lax.axis_index(TENSOR) * share
    kept = lax.dynamic_slice_in_dim(inputs, start, share, 1).reshape(each, features).astype(jnp.float32)
    mixed = kept + jnp.sum(partial.astype(jnp.float32), axis=0)

    hidden = (mixed * mid_gain).astype(jnp.bfloat16)
    hidden = jnp.broadcast_to(hidden[None], (blocks, each, features))
    hidden = lax.all_to_all(hidden, TENSOR, 0, 0, tiled=True)
    ours, theirs = sum_to_owner(hidden, 1.0 / mid_gain, up_weight, False)
    total = ours + theirs.astype(jnp.float32)
    units = up_weight.shape[1]
    inverse = lax.rsqrt(jnp.sum(total[:, units:], axis=-1, keepdims=True) / D + EPS)
    gate = total[:, :units] * inverse
    fired = ffn_mask.reshape(each, units) * (gate / (1.0 + jnp.exp(-gate)))

    partial = gathered_product(fired.astype(jnp.bfloat16), down_weight)
    partial = lax.all_to_all(partial.reshape(blocks, each, features), TENSOR, 0, 0, tiled=True)
    final = mixed + jnp.sum(partial.astype(jnp.float32), axis=0)
    return final.astype(jnp.bfloat16).reshape(STEPS, share, features)


def solution(mesh):
    devices = mesh.devices.reshape(8, 2, 4, 4)
    inner = Mesh(devices, ("z", "core", "y", "x"))
    return jax.shard_map(
        on_device,
        mesh=inner,
        in_specs=(
            P(None, None, BATCH),
            P(BATCH),
            P(BATCH, TENSOR),
            P(TENSOR),
            P(BATCH, TENSOR, None, None),
            P(TENSOR),
            P(TENSOR, BATCH),
            P(BATCH),
            P(BATCH, TENSOR),
            P(TENSOR, BATCH),
            P(None, BATCH, TENSOR),
            P(None, BATCH, TENSOR),
        ),
        out_specs=P(None, TENSOR, BATCH),
        check_vma=False,
    )
```

```python
import functools

import jax
import jax.numpy as jnp
from jax import lax
from jax.experimental import pallas as pl
from jax.experimental.pallas import tpu as pltpu
from jax.sharding import Mesh
from jax.sharding import PartitionSpec as P

D = 8192
STEPS = 3
DH = 128
EPS = 1e-06
LANES = 128
CHAINS = 2
GATHER_CHAINS = 3
BATCH = ("z", "core")
TENSOR = ("y", "x")
VMEM = pltpu.CompilerParams(vmem_limit_bytes=14 * 1024 * 1024)


def edges_of(width, count):
    tiles = width // LANES
    cuts = [LANES * (tiles * i // count) for i in range(count + 1)]
    return list(zip(cuts[:-1], cuts[1:], strict=True))


def swap_cores(value):
    return lax.ppermute(value, "core", [(0, 1), (1, 0)])


def pass_on(value):
    zs = lax.axis_size("z")
    pairs = []
    for z in range(zs):
        pairs.append((2 * z, 2 * ((z + 1) % zs)))
        pairs.append((2 * z + 1, 2 * ((z - 1) % zs) + 1))
    return lax.ppermute(value, BATCH, pairs)


def pieces_of(sums, source):
    high = lax.reduce_precision(sums, 8, 7)
    middle = lax.reduce_precision(sums - high, 8, 7)
    low = sums - high - middle
    lane = lax.broadcasted_iota(jnp.int32, (sums.shape[0], LANES), 1) - 3 * source
    return jnp.where(lane == 0, high, jnp.where(lane == 1, middle, jnp.where(lane == 2, low, 0.0)))


def product_kernel(chips, first, which, place_ref, rows_ref, gain_ref, weight_ref, out_ref, picked_ref):
    width = weight_ref.shape[1]
    share = picked_ref.shape[0] // (2 * STEPS * chips)
    zs = rows_ref.shape[1] // (2 * share) if first else rows_ref.shape[0] // 2
    start, source = place_ref[which], place_ref[2]
    gain = gain_ref[...] if first else 1.0 / gain_ref[...]
    for c in range(chips):
        chip = start + c
        chip = jnp.where(chip >= zs, chip - zs, chip)
        for core in range(2):
            for step in range(STEPS):
                at = ((c * 2 + core) * STEPS + step) * share
                if first:
                    from_row = pl.multiple_of(chip * (2 * share) + core * share, share)
                    values = rows_ref[step, pl.ds(from_row, share), :].astype(jnp.float32)
                    picked_ref[at : at + share, :] = (values * gain).astype(jnp.bfloat16)
                else:
                    block = rows_ref[chip * 2 + core, step * share : (step + 1) * share, :]
                    picked_ref[at : at + share, :] = block
                    values = block.astype(jnp.float32) * gain
                squares = jnp.sum(values * values, axis=-1, keepdims=True)
                out_ref[at : at + share, width:] = pieces_of(squares, source).astype(out_ref.dtype)
    chunk = 256
    for at in range(0, width, chunk):
        out_ref[:, at : at + chunk] = jnp.dot(
            picked_ref[...], weight_ref[:, at : at + chunk], preferred_element_type=jnp.float32
        ).astype(out_ref.dtype)


def product(rows, gain, weight, chips, which, place, first):
    share = (rows.shape[1] // 16) if first else rows.shape[1] // STEPS
    count = chips * 2 * STEPS * share
    depth, width = weight.shape
    if first:
        rows = pltpu.with_memory_space_constraint(rows, pltpu.HBM)
        weight = pltpu.with_memory_space_constraint(weight, pltpu.HBM)
    out = pl.pallas_call(
        functools.partial(product_kernel, chips, first, which),
        in_specs=[pl.BlockSpec(memory_space=pltpu.SMEM)] + [pl.BlockSpec(memory_space=pltpu.VMEM)] * 3,
        out_specs=pl.BlockSpec(memory_space=pltpu.VMEM),
        out_shape=jax.ShapeDtypeStruct((count, width + LANES), jnp.bfloat16),
        scratch_shapes=[pltpu.VMEM((count, depth), jnp.bfloat16)],
        compiler_params=VMEM,
    )(place, rows, gain[None, :], weight)
    return out.reshape(chips, 2, STEPS * share, width + LANES)


def sum_to_owner(rows, gain, weight, place, ahead, first):
    half = lax.axis_size("z") // 2
    theirs = product(rows, gain, weight, half, 0, place, first)
    got = swap_cores(theirs)
    mine = product(rows, gain, weight, half + 1, 1, place, first)

    def at(distance):
        own = jnp.where(ahead, mine[distance], mine[half - distance]).astype(jnp.float32)
        other = jnp.where(ahead, got[distance - 1], got[half - distance]).astype(jnp.float32)
        return own + other

    width = mine.shape[-1]
    edges = edges_of(width, CHAINS)
    which = (lax.broadcasted_iota(jnp.int32, (2, 1, 1), 0) == 0) == ahead
    farthest = at(half)
    carried = jnp.where(ahead, farthest[0], farthest[1]).astype(jnp.bfloat16)
    carried = [pass_on(carried[:, low:high]) for low, high in edges]
    parts = at(half - 1)
    totals = [
        parts[..., low:high] + jnp.where(which, part.astype(jnp.float32)[None], 0.0)
        for (low, high), part in zip(edges, carried, strict=True)
    ]
    for distance in range(half - 2, -1, -1):
        carried = [pass_on(total.astype(jnp.bfloat16)).astype(jnp.float32) for total in totals]
        parts = at(distance) if distance > 0 else jnp.where(ahead, mine[0], mine[half]).astype(jnp.float32)
        totals = [parts[..., low:high] + part for (low, high), part in zip(edges, carried, strict=True)]
    away = [swap_cores(jnp.where(ahead, total[1], total[0]).astype(jnp.bfloat16)) for total in totals]
    ours = [jnp.where(ahead, total[0], total[1]) for total in totals]
    return jnp.concatenate(ours, axis=-1), jnp.concatenate(away, axis=-1)


def attention_kernel(decay_ref, ours_ref, our_sums_ref, theirs_ref, their_sums_ref, state_ref, gain_ref, mask_ref, out_ref):
    head = pl.program_id(0)
    rows = ours_ref.shape[0]
    mine = rows // STEPS
    squares = jnp.sum(our_sums_ref[...] + their_sums_ref[...].astype(jnp.float32), axis=-1, keepdims=True)
    parts = (ours_ref[...] + theirs_ref[...].astype(jnp.float32)) * lax.rsqrt(squares / D + EPS)
    scale = DH ** (-0.5)
    queries = parts[:, :DH] * scale
    keys = parts[:, DH : 2 * DH] * scale
    values = parts[:, 2 * DH :]
    rate = decay_ref[head]
    turned = queries.T
    found = [[] for _ in range(STEPS)]
    for request in range(mine):
        block = state_ref[request, 0]
        for step in range(STEPS):
            at = step * mine + request
            found[step].append(jnp.sum(turned[:, at : at + 1] * block, axis=0, keepdims=True))
    power = rate
    for step in range(STEPS):
        here = slice(step * mine, (step + 1) * mine)
        total = power * jnp.concatenate(found[step], axis=0)
        power = power * rate
        factor = None
        for earlier in range(step, -1, -1):
            there = slice(earlier * mine, (earlier + 1) * mine)
            score = jnp.sum(queries[here] * keys[there], axis=-1, keepdims=True)
            if factor is not None:
                score = score * factor
            total = total + score * values[there]
            factor = rate if factor is None else factor * rate
        total = total * lax.rsqrt(jnp.mean(total * total, axis=-1, keepdims=True) + EPS)
        spiked = total * gain_ref[...] * mask_ref[step].astype(jnp.float32)
        out_ref[here, :] = spiked.astype(jnp.bfloat16)


def attention(decay, ours, theirs, state, head_gain, att_mask):
    rows, width = ours.shape
    mine, heads = state.shape[:2]
    last = width // LANES - 1
    return pl.pallas_call(
        attention_kernel,
        grid=(heads,),
        in_specs=[
            pl.BlockSpec(memory_space=pltpu.SMEM),
            pl.BlockSpec((rows, 3 * DH), lambda h: (0, h)),
            pl.BlockSpec((rows, LANES), lambda h: (0, last)),
            pl.BlockSpec((rows, 3 * DH), lambda h: (0, h)),
            pl.BlockSpec((rows, LANES), lambda h: (0, last)),
            pl.BlockSpec((mine, 1, DH, DH), lambda h: (0, h, 0, 0)),
            pl.BlockSpec((1, DH), lambda h: (0, h)),
            pl.BlockSpec((STEPS, mine, DH), lambda h: (0, 0, h)),
        ],
        out_specs=pl.BlockSpec((rows, DH), lambda h: (0, h)),
        out_shape=jax.ShapeDtypeStruct((rows, heads * DH), jnp.bfloat16),
        compiler_params=VMEM,
    )(decay, ours, ours, theirs, theirs, pltpu.with_memory_space_constraint(state, pltpu.HBM), head_gain[None, :], att_mask)


def mix_kernel(place_ref, partial_ref, inputs_ref, gain_ref, mixed_ref, hidden_ref):
    share = inputs_ref.shape[1]
    for step in range(STEPS):
        here = slice(step * share, (step + 1) * share)
        total = inputs_ref[step].astype(jnp.float32)
        for source in range(partial_ref.shape[0]):
            total = total + partial_ref[source, here, :].astype(jnp.float32)
        mixed_ref[here, :] = total
        hidden = (total * gain_ref[...]).astype(jnp.bfloat16)
        for target in range(hidden_ref.shape[0]):
            hidden_ref[target, here, :] = hidden


def mix(place, partial, inputs, gain):
    blocks, each, features = partial.shape
    whole = pl.BlockSpec((blocks, each, features), lambda i, place: (0, 0, 0))
    return pl.pallas_call(
        mix_kernel,
        grid_spec=pltpu.PrefetchScalarGridSpec(
            num_scalar_prefetch=1,
            grid=(1,),
            in_specs=[
                whole,
                pl.BlockSpec((STEPS, each // STEPS, features), lambda i, place: (0, place[3], 0)),
                pl.BlockSpec((1, features), lambda i, place: (0, 0)),
            ],
            out_specs=[pl.BlockSpec((each, features), lambda i, place: (0, 0)), whole],
        ),
        out_shape=[
            jax.ShapeDtypeStruct((each, features), jnp.float32),
            jax.ShapeDtypeStruct(partial.shape, jnp.bfloat16),
        ],
        compiler_params=VMEM,
    )(place, partial, pltpu.with_memory_space_constraint(inputs, pltpu.HBM), gain[None, :])


def gathered_product(value, weight):
    zs = lax.axis_size("z")
    half = zs // 2
    z, core = lax.axis_index("z"), lax.axis_index("core")
    towards = jnp.where(core == 0, -1, 1)
    rows, width = value.shape[0], weight.shape[1]
    out = jnp.zeros((zs, 2, rows, width), jnp.bfloat16)

    def multiply(blocks):
        return jnp.dot(blocks.reshape(-1, blocks.shape[-1]), weight, preferred_element_type=jnp.float32).astype(
            jnp.bfloat16
        ).reshape(blocks.shape[:-1] + (width,))

    def put(out, blocks, chip):
        return lax.dynamic_update_slice(out, blocks[None], ((chip + zs) % zs, 0, 0, 0))

    sibling = swap_cores(value)
    low, high = jnp.where(core == 0, value, sibling), jnp.where(core == 0, sibling, value)
    moving = jnp.stack([low, high])
    edges = edges_of(value.shape[1], GATHER_CHAINS)
    moving = [moving[..., low:high] for low, high in edges]
    weights = [weight[low:high] for low, high in edges]

    def multiply(blocks):
        total = 0.0
        for block, part in zip(blocks, weights, strict=True):
            total = total + jnp.dot(block.reshape(-1, block.shape[-1]), part, preferred_element_type=jnp.float32)
        return total.astype(jnp.bfloat16).reshape(blocks[0].shape[:-1] + (width,))

    out = put(out, multiply(moving), z)
    for distance in range(1, half):
        moving = [pass_on(part) for part in moving]
        other = [swap_cores(part) for part in moving]
        done = multiply([jnp.stack([a, b]) for a, b in zip(moving, other, strict=True)])
        out = put(out, done[0], z + towards * distance)
        out = put(out, done[1], z - towards * distance)
    return put(out, multiply([pass_on(part) for part in moving]), z + half)


def on_device(
    inputs,
    in_gain,
    qkv_weight,
    decay,
    state,
    head_gain,
    out_weight,
    mid_gain,
    up_weight,
    down_weight,
    att_mask,
    ffn_mask,
):
    blocks = lax.axis_size("core") * lax.axis_size("z")
    share = inputs.shape[1] // blocks
    features = inputs.shape[2]
    each = STEPS * share
    zs = lax.axis_size("z")
    z, core = lax.axis_index("z"), lax.axis_index("core")
    ahead = core == 0
    theirs_from = jnp.where(ahead, z + zs // 2, z + 1) % zs
    mine_from = jnp.where(ahead, z, z + zs // 2) % zs
    place = jnp.stack([theirs_from, mine_from, z * 2 + core, lax.axis_index(TENSOR)]).astype(jnp.int32)
    ours, theirs = sum_to_owner(inputs, in_gain, qkv_weight, place, ahead, True)
    spiked = attention(decay, ours, theirs, state, head_gain, att_mask)

    everyone = lax.all_gather(spiked, BATCH, axis=0, tiled=True)
    partial = jnp.dot(everyone, out_weight, preferred_element_type=jnp.float32).astype(jnp.bfloat16)
    partial = partial.reshape(blocks, each, features)
    partial = lax.all_to_all(partial, TENSOR, 0, 0, tiled=True)
    mixed, hidden = mix(place, partial, inputs, mid_gain)
    hidden = lax.all_to_all(hidden, TENSOR, 0, 0, tiled=True)
    ours, theirs = sum_to_owner(hidden, mid_gain, up_weight, place, ahead, False)
    total = ours + theirs.astype(jnp.float32)
    units = up_weight.shape[1]
    inverse = lax.rsqrt(jnp.sum(total[:, units:], axis=-1, keepdims=True) / D + EPS)
    gate = total[:, :units] * inverse
    fired = ffn_mask.reshape(each, units) * (gate / (1.0 + jnp.exp(-gate)))

    partial = gathered_product(fired.astype(jnp.bfloat16), down_weight)
    partial = lax.all_to_all(partial.reshape(blocks, each, features), TENSOR, 0, 0, tiled=True)
    final = mixed + jnp.sum(partial.astype(jnp.float32), axis=0)
    return final.astype(jnp.bfloat16).reshape(STEPS, share, features)


def solution(mesh):
    devices = mesh.devices.reshape(8, 2, 4, 4)
    inner = Mesh(devices, ("z", "core", "y", "x"))
    return jax.shard_map(
        on_device,
        mesh=inner,
        in_specs=(
            P(None, None, BATCH),
            P(BATCH),
            P(BATCH, TENSOR),
            P(TENSOR),
            P(BATCH, TENSOR, None, None),
            P(TENSOR),
            P(TENSOR, BATCH),
            P(BATCH),
            P(BATCH, TENSOR),
            P(TENSOR, BATCH),
            P(None, BATCH, TENSOR),
            P(None, BATCH, TENSOR),
        ),
        out_specs=P(None, TENSOR, BATCH),
        check_vma=False,
    )
```

```python
import functools

import jax
import jax.numpy as jnp
from jax import lax
from jax.experimental import pallas as pl
from jax.experimental.pallas import tpu as pltpu
from jax.sharding import Mesh
from jax.sharding import PartitionSpec as P

D = 8192
STEPS = 3
DH = 128
EPS = 1e-06
LANES = 128
CHAINS = 2
GATHER_CHAINS = 2
BATCH = ("z", "core")
TENSOR = ("y", "x")
VMEM = pltpu.CompilerParams(vmem_limit_bytes=14 * 1024 * 1024)


def edges_of(width, count):
    tiles = width // LANES
    cuts = [LANES * (tiles * i // count) for i in range(count + 1)]
    return list(zip(cuts[:-1], cuts[1:], strict=True))


def swap_cores(value):
    return lax.ppermute(value, "core", [(0, 1), (1, 0)])


def pass_on(value):
    zs = lax.axis_size("z")
    pairs = []
    for z in range(zs):
        pairs.append((2 * z, 2 * ((z + 1) % zs)))
        pairs.append((2 * z + 1, 2 * ((z - 1) % zs) + 1))
    return lax.ppermute(value, BATCH, pairs)


def pieces_of(sums, source):
    high = lax.reduce_precision(sums, 8, 7)
    middle = lax.reduce_precision(sums - high, 8, 7)
    low = sums - high - middle
    lane = lax.broadcasted_iota(jnp.int32, (sums.shape[0], LANES), 1) - 3 * source
    return jnp.where(lane == 0, high, jnp.where(lane == 1, middle, jnp.where(lane == 2, low, 0.0)))


def product_kernel(chips, first, which, place_ref, rows_ref, gain_ref, weight_ref, out_ref, picked_ref):
    width = weight_ref.shape[1]
    share = picked_ref.shape[0] // (2 * STEPS * chips)
    zs = rows_ref.shape[1] // (2 * share) if first else rows_ref.shape[0] // 2
    start, source = place_ref[which], place_ref[2]
    gain = gain_ref[...] if first else 1.0 / gain_ref[...]
    for c in range(chips):
        chip = start + c
        chip = jnp.where(chip >= zs, chip - zs, chip)
        for core in range(2):
            for step in range(STEPS):
                at = ((c * 2 + core) * STEPS + step) * share
                if first:
                    from_row = pl.multiple_of(chip * (2 * share) + core * share, share)
                    values = rows_ref[step, pl.ds(from_row, share), :].astype(jnp.float32)
                    picked_ref[at : at + share, :] = (values * gain).astype(jnp.bfloat16)
                else:
                    block = rows_ref[chip * 2 + core, step * share : (step + 1) * share, :]
                    picked_ref[at : at + share, :] = block
                    values = block.astype(jnp.float32) * gain
                squares = jnp.sum(values * values, axis=-1, keepdims=True)
                out_ref[at : at + share, width:] = pieces_of(squares, source).astype(out_ref.dtype)
    chunk = 256
    for at in range(0, width, chunk):
        out_ref[:, at : at + chunk] = jnp.dot(
            picked_ref[...], weight_ref[:, at : at + chunk], preferred_element_type=jnp.float32
        ).astype(out_ref.dtype)


def product(rows, gain, weight, chips, which, place, first):
    share = (rows.shape[1] // 16) if first else rows.shape[1] // STEPS
    count = chips * 2 * STEPS * share
    depth, width = weight.shape
    if first:
        rows = pltpu.with_memory_space_constraint(rows, pltpu.HBM)
        weight = pltpu.with_memory_space_constraint(weight, pltpu.HBM)
    out = pl.pallas_call(
        functools.partial(product_kernel, chips, first, which),
        in_specs=[pl.BlockSpec(memory_space=pltpu.SMEM)] + [pl.BlockSpec(memory_space=pltpu.VMEM)] * 3,
        out_specs=pl.BlockSpec(memory_space=pltpu.VMEM),
        out_shape=jax.ShapeDtypeStruct((count, width + LANES), jnp.bfloat16),
        scratch_shapes=[pltpu.VMEM((count, depth), jnp.bfloat16)],
        compiler_params=VMEM,
    )(place, rows, gain[None, :], weight)
    return out.reshape(chips, 2, STEPS * share, width + LANES)


def sum_to_owner(rows, gain, weight, place, ahead, first):
    half = lax.axis_size("z") // 2
    theirs = product(rows, gain, weight, half, 0, place, first)
    got = swap_cores(theirs)
    mine = product(rows, gain, weight, half + 1, 1, place, first)

    def at(distance):
        own = jnp.where(ahead, mine[distance], mine[half - distance]).astype(jnp.float32)
        other = jnp.where(ahead, got[distance - 1], got[half - distance]).astype(jnp.float32)
        return own + other

    width = mine.shape[-1]
    edges = edges_of(width, CHAINS)
    which = (lax.broadcasted_iota(jnp.int32, (2, 1, 1), 0) == 0) == ahead
    farthest = at(half)
    carried = jnp.where(ahead, farthest[0], farthest[1]).astype(jnp.bfloat16)
    carried = [pass_on(carried[:, low:high]) for low, high in edges]
    parts = at(half - 1)
    totals = [
        parts[..., low:high] + jnp.where(which, part.astype(jnp.float32)[None], 0.0)
        for (low, high), part in zip(edges, carried, strict=True)
    ]
    for distance in range(half - 2, -1, -1):
        carried = [pass_on(total.astype(jnp.bfloat16)).astype(jnp.float32) for total in totals]
        parts = at(distance) if distance > 0 else jnp.where(ahead, mine[0], mine[half]).astype(jnp.float32)
        totals = [parts[..., low:high] + part for (low, high), part in zip(edges, carried, strict=True)]
    away = [swap_cores(jnp.where(ahead, total[1], total[0]).astype(jnp.bfloat16)) for total in totals]
    ours = [jnp.where(ahead, total[0], total[1]) for total in totals]
    return jnp.concatenate(ours, axis=-1), jnp.concatenate(away, axis=-1)


def attention_kernel(decay_ref, ours_ref, our_sums_ref, theirs_ref, their_sums_ref, state_ref, gain_ref, mask_ref, out_ref):
    head = pl.program_id(0)
    rows = ours_ref.shape[0]
    mine = rows // STEPS
    squares = jnp.sum(our_sums_ref[...] + their_sums_ref[...].astype(jnp.float32), axis=-1, keepdims=True)
    parts = (ours_ref[...] + theirs_ref[...].astype(jnp.float32)) * lax.rsqrt(squares / D + EPS)
    scale = DH ** (-0.5)
    queries = parts[:, :DH] * scale
    keys = parts[:, DH : 2 * DH] * scale
    values = parts[:, 2 * DH :]
    rate = decay_ref[head]
    turned = queries.T
    found = [[] for _ in range(STEPS)]
    for request in range(mine):
        block = state_ref[request, 0]
        for step in range(STEPS):
            at = step * mine + request
            found[step].append(jnp.sum(turned[:, at : at + 1] * block, axis=0, keepdims=True))
    power = rate
    for step in range(STEPS):
        here = slice(step * mine, (step + 1) * mine)
        total = power * jnp.concatenate(found[step], axis=0)
        power = power * rate
        factor = None
        for earlier in range(step, -1, -1):
            there = slice(earlier * mine, (earlier + 1) * mine)
            score = jnp.sum(queries[here] * keys[there], axis=-1, keepdims=True)
            if factor is not None:
                score = score * factor
            total = total + score * values[there]
            factor = rate if factor is None else factor * rate
        total = total * lax.rsqrt(jnp.mean(total * total, axis=-1, keepdims=True) + EPS)
        spiked = total * gain_ref[...] * mask_ref[step].astype(jnp.float32)
        out_ref[here, :] = spiked.astype(jnp.bfloat16)


def attention(decay, ours, theirs, state, head_gain, att_mask):
    rows, width = ours.shape
    mine, heads = state.shape[:2]
    last = width // LANES - 1
    return pl.pallas_call(
        attention_kernel,
        grid=(heads,),
        in_specs=[
            pl.BlockSpec(memory_space=pltpu.SMEM),
            pl.BlockSpec((rows, 3 * DH), lambda h: (0, h)),
            pl.BlockSpec((rows, LANES), lambda h: (0, last)),
            pl.BlockSpec((rows, 3 * DH), lambda h: (0, h)),
            pl.BlockSpec((rows, LANES), lambda h: (0, last)),
            pl.BlockSpec((mine, 1, DH, DH), lambda h: (0, h, 0, 0)),
            pl.BlockSpec((1, DH), lambda h: (0, h)),
            pl.BlockSpec((STEPS, mine, DH), lambda h: (0, 0, h)),
        ],
        out_specs=pl.BlockSpec((rows, DH), lambda h: (0, h)),
        out_shape=jax.ShapeDtypeStruct((rows, heads * DH), jnp.bfloat16),
        compiler_params=VMEM,
    )(decay, ours, ours, theirs, theirs, pltpu.with_memory_space_constraint(state, pltpu.HBM), head_gain[None, :], att_mask)


def mix_kernel(place_ref, partial_ref, inputs_ref, gain_ref, mixed_ref, hidden_ref):
    share = inputs_ref.shape[1]
    for step in range(STEPS):
        here = slice(step * share, (step + 1) * share)
        total = inputs_ref[step].astype(jnp.float32)
        for source in range(partial_ref.shape[0]):
            total = total + partial_ref[source, here, :].astype(jnp.float32)
        mixed_ref[here, :] = total
        hidden = (total * gain_ref[...]).astype(jnp.bfloat16)
        for target in range(hidden_ref.shape[0]):
            hidden_ref[target, here, :] = hidden


def mix(place, partial, inputs, gain):
    blocks, each, features = partial.shape
    whole = pl.BlockSpec((blocks, each, features), lambda i, place: (0, 0, 0))
    return pl.pallas_call(
        mix_kernel,
        grid_spec=pltpu.PrefetchScalarGridSpec(
            num_scalar_prefetch=1,
            grid=(1,),
            in_specs=[
                whole,
                pl.BlockSpec((STEPS, each // STEPS, features), lambda i, place: (0, place[3], 0)),
                pl.BlockSpec((1, features), lambda i, place: (0, 0)),
            ],
            out_specs=[pl.BlockSpec((each, features), lambda i, place: (0, 0)), whole],
        ),
        out_shape=[
            jax.ShapeDtypeStruct((each, features), jnp.float32),
            jax.ShapeDtypeStruct(partial.shape, jnp.bfloat16),
        ],
        compiler_params=VMEM,
    )(place, partial, pltpu.with_memory_space_constraint(inputs, pltpu.HBM), gain[None, :])


def gathered_product(value, weight):
    zs = lax.axis_size("z")
    half = zs // 2
    z, core = lax.axis_index("z"), lax.axis_index("core")
    towards = jnp.where(core == 0, -1, 1)
    rows, width = value.shape[0], weight.shape[1]
    out = jnp.zeros((zs, 2, rows, width), jnp.bfloat16)

    def multiply(blocks):
        return jnp.dot(blocks.reshape(-1, blocks.shape[-1]), weight, preferred_element_type=jnp.float32).astype(
            jnp.bfloat16
        ).reshape(blocks.shape[:-1] + (width,))

    def put(out, blocks, chip):
        return lax.dynamic_update_slice(out, blocks[None], ((chip + zs) % zs, 0, 0, 0))

    sibling = swap_cores(value)
    low, high = jnp.where(core == 0, value, sibling), jnp.where(core == 0, sibling, value)
    moving = jnp.stack([low, high])
    edges = edges_of(value.shape[1], GATHER_CHAINS)
    moving = [moving[..., low:high] for low, high in edges]
    weights = [weight[low:high] for low, high in edges]

    def multiply(blocks):
        total = 0.0
        for block, part in zip(blocks, weights, strict=True):
            total = total + jnp.dot(block.reshape(-1, block.shape[-1]), part, preferred_element_type=jnp.float32)
        return total.astype(jnp.bfloat16).reshape(blocks[0].shape[:-1] + (width,))

    out = put(out, multiply(moving), z)
    for distance in range(1, half):
        moving = [pass_on(part) for part in moving]
        other = [swap_cores(part) for part in moving]
        done = multiply([jnp.stack([a, b]) for a, b in zip(moving, other, strict=True)])
        out = put(out, done[0], z + towards * distance)
        out = put(out, done[1], z - towards * distance)
    return put(out, multiply([pass_on(part) for part in moving]), z + half)


def on_device(
    inputs,
    in_gain,
    qkv_weight,
    decay,
    state,
    head_gain,
    out_weight,
    mid_gain,
    up_weight,
    down_weight,
    att_mask,
    ffn_mask,
):
    blocks = lax.axis_size("core") * lax.axis_size("z")
    share = inputs.shape[1] // blocks
    features = inputs.shape[2]
    each = STEPS * share
    zs = lax.axis_size("z")
    z, core = lax.axis_index("z"), lax.axis_index("core")
    ahead = core == 0
    theirs_from = jnp.where(ahead, z + zs // 2, z + 1) % zs
    mine_from = jnp.where(ahead, z, z + zs // 2) % zs
    place = jnp.stack([theirs_from, mine_from, z * 2 + core, lax.axis_index(TENSOR)]).astype(jnp.int32)
    ours, theirs = sum_to_owner(inputs, in_gain, qkv_weight, place, ahead, True)
    spiked = attention(decay, ours, theirs, state, head_gain, att_mask)

    everyone = lax.all_gather(spiked, BATCH, axis=0, tiled=True)
    partial = jnp.dot(everyone, out_weight, preferred_element_type=jnp.float32).astype(jnp.bfloat16)
    partial = partial.reshape(blocks, each, features)
    partial = lax.all_to_all(partial, TENSOR, 0, 0, tiled=True)
    mixed, hidden = mix(place, partial, inputs, mid_gain)
    hidden = lax.all_to_all(hidden, TENSOR, 0, 0, tiled=True)
    ours, theirs = sum_to_owner(hidden, mid_gain, up_weight, place, ahead, False)
    total = ours + theirs.astype(jnp.float32)
    units = up_weight.shape[1]
    inverse = lax.rsqrt(jnp.sum(total[:, units:], axis=-1, keepdims=True) / D + EPS)
    gate = total[:, :units] * inverse
    fired = ffn_mask.reshape(each, units) * (gate / (1.0 + jnp.exp(-gate)))

    partial = gathered_product(fired.astype(jnp.bfloat16), down_weight)
    partial = lax.all_to_all(partial.reshape(blocks, each, features), TENSOR, 0, 0, tiled=True)
    final = mixed + jnp.sum(partial.astype(jnp.float32), axis=0)
    return final.astype(jnp.bfloat16).reshape(STEPS, share, features)


def solution(mesh):
    devices = mesh.devices.reshape(8, 2, 4, 4)
    inner = Mesh(devices, ("z", "core", "y", "x"))
    return jax.shard_map(
        on_device,
        mesh=inner,
        in_specs=(
            P(None, None, BATCH),
            P(BATCH),
            P(BATCH, TENSOR),
            P(TENSOR),
            P(BATCH, TENSOR, None, None),
            P(TENSOR),
            P(TENSOR, BATCH),
            P(BATCH),
            P(BATCH, TENSOR),
            P(TENSOR, BATCH),
            P(None, BATCH, TENSOR),
            P(None, BATCH, TENSOR),
        ),
        out_specs=P(None, TENSOR, BATCH),
        check_vma=False,
    )
```

```python
import functools

import jax
import jax.numpy as jnp
from jax import lax
from jax.experimental import pallas as pl
from jax.experimental.pallas import tpu as pltpu
from jax.sharding import Mesh
from jax.sharding import PartitionSpec as P

D = 8192
STEPS = 3
DH = 128
EPS = 1e-06
LANES = 128
CHAINS = 2
GATHER_CHAINS = 2
BATCH = ("z", "core")
TENSOR = ("y", "x")
VMEM = pltpu.CompilerParams(vmem_limit_bytes=14 * 1024 * 1024)


def edges_of(width, count):
    tiles = width // LANES
    cuts = [LANES * (tiles * i // count) for i in range(count + 1)]
    return list(zip(cuts[:-1], cuts[1:], strict=True))


def swap_cores(value):
    return lax.ppermute(value, "core", [(0, 1), (1, 0)])


def pass_on(value):
    zs = lax.axis_size("z")
    pairs = []
    for z in range(zs):
        pairs.append((2 * z, 2 * ((z + 1) % zs)))
        pairs.append((2 * z + 1, 2 * ((z - 1) % zs) + 1))
    return lax.ppermute(value, BATCH, pairs)


def pieces_of(sums, source):
    high = lax.reduce_precision(sums, 8, 7)
    middle = lax.reduce_precision(sums - high, 8, 7)
    low = sums - high - middle
    lane = lax.broadcasted_iota(jnp.int32, (sums.shape[0], LANES), 1) - 3 * source
    return jnp.where(lane == 0, high, jnp.where(lane == 1, middle, jnp.where(lane == 2, low, 0.0)))


def product_kernel(chips, first, which, place_ref, rows_ref, gain_ref, weight_ref, out_ref, picked_ref):
    width = weight_ref.shape[1]
    share = picked_ref.shape[0] // (2 * STEPS * chips)
    zs = rows_ref.shape[1] // (2 * share) if first else rows_ref.shape[0] // 2
    start, source = place_ref[which], place_ref[2]
    gain = gain_ref[...] if first else 1.0 / gain_ref[...]
    for c in range(chips):
        chip = start + c
        chip = jnp.where(chip >= zs, chip - zs, chip)
        for core in range(2):
            for step in range(STEPS):
                at = ((c * 2 + core) * STEPS + step) * share
                if first:
                    from_row = pl.multiple_of(chip * (2 * share) + core * share, share)
                    values = rows_ref[step, pl.ds(from_row, share), :].astype(jnp.float32)
                    picked_ref[at : at + share, :] = (values * gain).astype(jnp.bfloat16)
                else:
                    block = rows_ref[chip * 2 + core, step * share : (step + 1) * share, :]
                    picked_ref[at : at + share, :] = block
                    values = block.astype(jnp.float32) * gain
                squares = jnp.sum(values * values, axis=-1, keepdims=True)
                out_ref[at : at + share, width:] = pieces_of(squares, source).astype(out_ref.dtype)
    chunk = 256
    for at in range(0, width, chunk):
        out_ref[:, at : at + chunk] = jnp.dot(
            picked_ref[...], weight_ref[:, at : at + chunk], preferred_element_type=jnp.float32
        ).astype(out_ref.dtype)


def product(rows, gain, weight, chips, which, place, first):
    share = (rows.shape[1] // 16) if first else rows.shape[1] // STEPS
    count = chips * 2 * STEPS * share
    depth, width = weight.shape
    if first:
        rows = pltpu.with_memory_space_constraint(rows, pltpu.HBM)
        weight = pltpu.with_memory_space_constraint(weight, pltpu.HBM)
    out = pl.pallas_call(
        functools.partial(product_kernel, chips, first, which),
        in_specs=[pl.BlockSpec(memory_space=pltpu.SMEM)] + [pl.BlockSpec(memory_space=pltpu.VMEM)] * 3,
        out_specs=pl.BlockSpec(memory_space=pltpu.VMEM),
        out_shape=jax.ShapeDtypeStruct((count, width + LANES), jnp.bfloat16),
        scratch_shapes=[pltpu.VMEM((count, depth), jnp.bfloat16)],
        compiler_params=VMEM,
    )(place, rows, gain[None, :], weight)
    return out.reshape(chips, 2, STEPS * share, width + LANES)


def sum_to_owner(rows, gain, weight, place, ahead, first):
    half = lax.axis_size("z") // 2
    theirs = product(rows, gain, weight, half, 0, place, first)
    got = swap_cores(theirs)
    mine = product(rows, gain, weight, half + 1, 1, place, first)

    def at(distance):
        own = jnp.where(ahead, mine[distance], mine[half - distance]).astype(jnp.float32)
        other = jnp.where(ahead, got[distance - 1], got[half - distance]).astype(jnp.float32)
        return own + other

    width = mine.shape[-1]
    edges = edges_of(width, CHAINS)
    which = (lax.broadcasted_iota(jnp.int32, (2, 1, 1), 0) == 0) == ahead
    farthest = at(half)
    carried = jnp.where(ahead, farthest[0], farthest[1]).astype(jnp.bfloat16)
    carried = [pass_on(carried[:, low:high]) for low, high in edges]
    parts = at(half - 1)
    totals = [
        parts[..., low:high] + jnp.where(which, part.astype(jnp.float32)[None], 0.0)
        for (low, high), part in zip(edges, carried, strict=True)
    ]
    for distance in range(half - 2, -1, -1):
        carried = [pass_on(total.astype(jnp.bfloat16)).astype(jnp.float32) for total in totals]
        parts = at(distance) if distance > 0 else jnp.where(ahead, mine[0], mine[half]).astype(jnp.float32)
        totals = [parts[..., low:high] + part for (low, high), part in zip(edges, carried, strict=True)]
    away = [swap_cores(jnp.where(ahead, total[1], total[0]).astype(jnp.bfloat16)) for total in totals]
    ours = [jnp.where(ahead, total[0], total[1]) for total in totals]
    return jnp.concatenate(ours, axis=-1), jnp.concatenate(away, axis=-1)


def attention_kernel(decay_ref, ours_ref, our_sums_ref, theirs_ref, their_sums_ref, state_ref, gain_ref, mask_ref, out_ref):
    head = pl.program_id(0)
    rows = ours_ref.shape[0]
    mine = rows // STEPS
    squares = jnp.sum(our_sums_ref[...] + their_sums_ref[...].astype(jnp.float32), axis=-1, keepdims=True)
    parts = (ours_ref[...] + theirs_ref[...].astype(jnp.float32)) * lax.rsqrt(squares / D + EPS)
    scale = DH ** (-0.5)
    queries = parts[:, :DH] * scale
    keys = parts[:, DH : 2 * DH] * scale
    values = parts[:, 2 * DH :]
    rate = decay_ref[head]
    tiled = jnp.concatenate([queries] * mine, axis=1)
    row = lax.broadcasted_iota(jnp.int32, tiled.shape, 0) % mine
    column = lax.broadcasted_iota(jnp.int32, tiled.shape, 1) // DH
    left = jnp.where(row == column, tiled, 0.0)
    left_high = left.astype(jnp.bfloat16)
    left_low = (left - left_high.astype(jnp.float32)).astype(jnp.bfloat16)
    right = state_ref[...].reshape(mine * DH, DH)
    right_high = right.astype(jnp.bfloat16)
    right_low = (right - right_high.astype(jnp.float32)).astype(jnp.bfloat16)
    both = jnp.concatenate([left_high, left_low], axis=0)
    found = jnp.dot(both, right_high, preferred_element_type=jnp.float32)
    found = found[:rows] + found[rows:] + jnp.dot(left_high, right_low, preferred_element_type=jnp.float32)
    power = rate
    for step in range(STEPS):
        here = slice(step * mine, (step + 1) * mine)
        total = power * found[here]
        power = power * rate
        factor = None
        for earlier in range(step, -1, -1):
            there = slice(earlier * mine, (earlier + 1) * mine)
            score = jnp.sum(queries[here] * keys[there], axis=-1, keepdims=True)
            if factor is not None:
                score = score * factor
            total = total + score * values[there]
            factor = rate if factor is None else factor * rate
        total = total * lax.rsqrt(jnp.mean(total * total, axis=-1, keepdims=True) + EPS)
        spiked = total * gain_ref[...] * mask_ref[step].astype(jnp.float32)
        out_ref[here, :] = spiked.astype(jnp.bfloat16)


def attention(decay, ours, theirs, state, head_gain, att_mask):
    rows, width = ours.shape
    mine, heads = state.shape[:2]
    last = width // LANES - 1
    return pl.pallas_call(
        attention_kernel,
        grid=(heads,),
        in_specs=[
            pl.BlockSpec(memory_space=pltpu.SMEM),
            pl.BlockSpec((rows, 3 * DH), lambda h: (0, h)),
            pl.BlockSpec((rows, LANES), lambda h: (0, last)),
            pl.BlockSpec((rows, 3 * DH), lambda h: (0, h)),
            pl.BlockSpec((rows, LANES), lambda h: (0, last)),
            pl.BlockSpec((mine, 1, DH, DH), lambda h: (0, h, 0, 0)),
            pl.BlockSpec((1, DH), lambda h: (0, h)),
            pl.BlockSpec((STEPS, mine, DH), lambda h: (0, 0, h)),
        ],
        out_specs=pl.BlockSpec((rows, DH), lambda h: (0, h)),
        out_shape=jax.ShapeDtypeStruct((rows, heads * DH), jnp.bfloat16),
        compiler_params=VMEM,
    )(decay, ours, ours, theirs, theirs, pltpu.with_memory_space_constraint(state, pltpu.HBM), head_gain[None, :], att_mask)


def mix_kernel(place_ref, partial_ref, inputs_ref, gain_ref, mixed_ref, hidden_ref):
    share = inputs_ref.shape[1]
    for step in range(STEPS):
        here = slice(step * share, (step + 1) * share)
        total = inputs_ref[step].astype(jnp.float32)
        for source in range(partial_ref.shape[0]):
            total = total + partial_ref[source, here, :].astype(jnp.float32)
        mixed_ref[here, :] = total
        hidden = (total * gain_ref[...]).astype(jnp.bfloat16)
        for target in range(hidden_ref.shape[0]):
            hidden_ref[target, here, :] = hidden


def mix(place, partial, inputs, gain):
    blocks, each, features = partial.shape
    whole = pl.BlockSpec((blocks, each, features), lambda i, place: (0, 0, 0))
    return pl.pallas_call(
        mix_kernel,
        grid_spec=pltpu.PrefetchScalarGridSpec(
            num_scalar_prefetch=1,
            grid=(1,),
            in_specs=[
                whole,
                pl.BlockSpec((STEPS, each // STEPS, features), lambda i, place: (0, place[3], 0)),
                pl.BlockSpec((1, features), lambda i, place: (0, 0)),
            ],
            out_specs=[pl.BlockSpec((each, features), lambda i, place: (0, 0)), whole],
        ),
        out_shape=[
            jax.ShapeDtypeStruct((each, features), jnp.float32),
            jax.ShapeDtypeStruct(partial.shape, jnp.bfloat16),
        ],
        compiler_params=VMEM,
    )(place, partial, pltpu.with_memory_space_constraint(inputs, pltpu.HBM), gain[None, :])


def gathered_product(value, weight):
    zs = lax.axis_size("z")
    half = zs // 2
    z, core = lax.axis_index("z"), lax.axis_index("core")
    towards = jnp.where(core == 0, -1, 1)
    rows, width = value.shape[0], weight.shape[1]
    out = jnp.zeros((zs, 2, rows, width), jnp.bfloat16)

    def multiply(blocks):
        return jnp.dot(blocks.reshape(-1, blocks.shape[-1]), weight, preferred_element_type=jnp.float32).astype(
            jnp.bfloat16
        ).reshape(blocks.shape[:-1] + (width,))

    def put(out, blocks, chip):
        return lax.dynamic_update_slice(out, blocks[None], ((chip + zs) % zs, 0, 0, 0))

    sibling = swap_cores(value)
    low, high = jnp.where(core == 0, value, sibling), jnp.where(core == 0, sibling, value)
    moving = jnp.stack([low, high])
    edges = edges_of(value.shape[1], GATHER_CHAINS)
    moving = [moving[..., low:high] for low, high in edges]
    weights = [weight[low:high] for low, high in edges]

    def multiply(blocks):
        total = 0.0
        for block, part in zip(blocks, weights, strict=True):
            total = total + jnp.dot(block.reshape(-1, block.shape[-1]), part, preferred_element_type=jnp.float32)
        return total.astype(jnp.bfloat16).reshape(blocks[0].shape[:-1] + (width,))

    out = put(out, multiply(moving), z)
    for distance in range(1, half):
        moving = [pass_on(part) for part in moving]
        other = [swap_cores(part) for part in moving]
        done = multiply([jnp.stack([a, b]) for a, b in zip(moving, other, strict=True)])
        out = put(out, done[0], z + towards * distance)
        out = put(out, done[1], z - towards * distance)
    return put(out, multiply([pass_on(part) for part in moving]), z + half)


def on_device(
    inputs,
    in_gain,
    qkv_weight,
    decay,
    state,
    head_gain,
    out_weight,
    mid_gain,
    up_weight,
    down_weight,
    att_mask,
    ffn_mask,
):
    blocks = lax.axis_size("core") * lax.axis_size("z")
    share = inputs.shape[1] // blocks
    features = inputs.shape[2]
    each = STEPS * share
    zs = lax.axis_size("z")
    z, core = lax.axis_index("z"), lax.axis_index("core")
    ahead = core == 0
    theirs_from = jnp.where(ahead, z + zs // 2, z + 1) % zs
    mine_from = jnp.where(ahead, z, z + zs // 2) % zs
    place = jnp.stack([theirs_from, mine_from, z * 2 + core, lax.axis_index(TENSOR)]).astype(jnp.int32)
    ours, theirs = sum_to_owner(inputs, in_gain, qkv_weight, place, ahead, True)
    spiked = attention(decay, ours, theirs, state, head_gain, att_mask)

    everyone = lax.all_gather(spiked, BATCH, axis=0, tiled=True)
    partial = jnp.dot(everyone, out_weight, preferred_element_type=jnp.float32).astype(jnp.bfloat16)
    partial = partial.reshape(blocks, each, features)
    partial = lax.all_to_all(partial, TENSOR, 0, 0, tiled=True)
    mixed, hidden = mix(place, partial, inputs, mid_gain)
    hidden = lax.all_to_all(hidden, TENSOR, 0, 0, tiled=True)
    ours, theirs = sum_to_owner(hidden, mid_gain, up_weight, place, ahead, False)
    total = ours + theirs.astype(jnp.float32)
    units = up_weight.shape[1]
    inverse = lax.rsqrt(jnp.sum(total[:, units:], axis=-1, keepdims=True) / D + EPS)
    gate = total[:, :units] * inverse
    fired = ffn_mask.reshape(each, units) * (gate / (1.0 + jnp.exp(-gate)))

    partial = gathered_product(fired.astype(jnp.bfloat16), down_weight)
    partial = lax.all_to_all(partial.reshape(blocks, each, features), TENSOR, 0, 0, tiled=True)
    final = mixed + jnp.sum(partial.astype(jnp.float32), axis=0)
    return final.astype(jnp.bfloat16).reshape(STEPS, share, features)


def solution(mesh):
    devices = mesh.devices.reshape(8, 2, 4, 4)
    inner = Mesh(devices, ("z", "core", "y", "x"))
    return jax.shard_map(
        on_device,
        mesh=inner,
        in_specs=(
            P(None, None, BATCH),
            P(BATCH),
            P(BATCH, TENSOR),
            P(TENSOR),
            P(BATCH, TENSOR, None, None),
            P(TENSOR),
            P(TENSOR, BATCH),
            P(BATCH),
            P(BATCH, TENSOR),
            P(TENSOR, BATCH),
            P(None, BATCH, TENSOR),
            P(None, BATCH, TENSOR),
        ),
        out_specs=P(None, TENSOR, BATCH),
        check_vma=False,
    )
```

```python
import functools

import jax
import jax.numpy as jnp
from jax import lax
from jax.experimental import pallas as pl
from jax.experimental.pallas import tpu as pltpu
from jax.sharding import Mesh
from jax.sharding import PartitionSpec as P

D = 8192
STEPS = 3
DH = 128
EPS = 1e-06
LANES = 128
CHAINS = 2
GATHER_CHAINS = 2
BATCH = ("z", "core")
TENSOR = ("y", "x")
VMEM = pltpu.CompilerParams(vmem_limit_bytes=14 * 1024 * 1024)


def edges_of(width, count):
    tiles = width // LANES
    cuts = [LANES * (tiles * i // count) for i in range(count + 1)]
    return list(zip(cuts[:-1], cuts[1:], strict=True))


def swap_cores(value):
    return lax.ppermute(value, "core", [(0, 1), (1, 0)])


def pass_on(value):
    zs = lax.axis_size("z")
    pairs = []
    for z in range(zs):
        pairs.append((2 * z, 2 * ((z + 1) % zs)))
        pairs.append((2 * z + 1, 2 * ((z - 1) % zs) + 1))
    return lax.ppermute(value, BATCH, pairs)


def pieces_of(sums, source):
    high = lax.reduce_precision(sums, 8, 7)
    middle = lax.reduce_precision(sums - high, 8, 7)
    low = sums - high - middle
    lane = lax.broadcasted_iota(jnp.int32, (sums.shape[0], LANES), 1) - 3 * source
    return jnp.where(lane == 0, high, jnp.where(lane == 1, middle, jnp.where(lane == 2, low, 0.0)))


def product_kernel(chips, first, which, place_ref, rows_ref, gain_ref, weight_ref, out_ref, picked_ref):
    width = weight_ref.shape[1]
    share = picked_ref.shape[0] // (2 * STEPS * chips)
    zs = rows_ref.shape[1] // (2 * share) if first else rows_ref.shape[0] // 2
    start, source = place_ref[which], place_ref[2]
    gain = gain_ref[...] if first else 1.0 / gain_ref[...]
    for c in range(chips):
        chip = start + c
        chip = jnp.where(chip >= zs, chip - zs, chip)
        for core in range(2):
            for step in range(STEPS):
                at = ((c * 2 + core) * STEPS + step) * share
                if first:
                    from_row = pl.multiple_of(chip * (2 * share) + core * share, share)
                    values = rows_ref[step, pl.ds(from_row, share), :].astype(jnp.float32)
                    picked_ref[at : at + share, :] = (values * gain).astype(jnp.bfloat16)
                else:
                    block = rows_ref[chip * 2 + core, step * share : (step + 1) * share, :]
                    picked_ref[at : at + share, :] = block
                    values = block.astype(jnp.float32) * gain
                squares = jnp.sum(values * values, axis=-1, keepdims=True)
                out_ref[at : at + share, width:] = pieces_of(squares, source).astype(out_ref.dtype)
    chunk = 256
    for at in range(0, width, chunk):
        out_ref[:, at : at + chunk] = jnp.dot(
            picked_ref[...], weight_ref[:, at : at + chunk], preferred_element_type=jnp.float32
        ).astype(out_ref.dtype)


def product(rows, gain, weight, chips, which, place, first):
    share = (rows.shape[1] // 16) if first else rows.shape[1] // STEPS
    count = chips * 2 * STEPS * share
    depth, width = weight.shape
    if first:
        rows = pltpu.with_memory_space_constraint(rows, pltpu.HBM)
        weight = pltpu.with_memory_space_constraint(weight, pltpu.HBM)
    out = pl.pallas_call(
        functools.partial(product_kernel, chips, first, which),
        in_specs=[pl.BlockSpec(memory_space=pltpu.SMEM)] + [pl.BlockSpec(memory_space=pltpu.VMEM)] * 3,
        out_specs=pl.BlockSpec(memory_space=pltpu.VMEM),
        out_shape=jax.ShapeDtypeStruct((count, width + LANES), jnp.bfloat16),
        scratch_shapes=[pltpu.VMEM((count, depth), jnp.bfloat16)],
        compiler_params=VMEM,
    )(place, rows, gain[None, :], weight)
    return out.reshape(chips, 2, STEPS * share, width + LANES)


def sum_to_owner(rows, gain, weight, place, ahead, first):
    half = lax.axis_size("z") // 2
    theirs = product(rows, gain, weight, half, 0, place, first)
    got = swap_cores(theirs)
    mine = product(rows, gain, weight, half + 1, 1, place, first)

    def at(distance):
        own = jnp.where(ahead, mine[distance], mine[half - distance]).astype(jnp.float32)
        other = jnp.where(ahead, got[distance - 1], got[half - distance]).astype(jnp.float32)
        return own + other

    width = mine.shape[-1]
    edges = edges_of(width, CHAINS)
    which = (lax.broadcasted_iota(jnp.int32, (2, 1, 1), 0) == 0) == ahead
    farthest = at(half)
    carried = jnp.where(ahead, farthest[0], farthest[1]).astype(jnp.bfloat16)
    carried = [pass_on(carried[:, low:high]) for low, high in edges]
    parts = at(half - 1)
    totals = [
        parts[..., low:high] + jnp.where(which, part.astype(jnp.float32)[None], 0.0)
        for (low, high), part in zip(edges, carried, strict=True)
    ]
    for distance in range(half - 2, -1, -1):
        carried = [pass_on(total.astype(jnp.bfloat16)).astype(jnp.float32) for total in totals]
        parts = at(distance) if distance > 0 else jnp.where(ahead, mine[0], mine[half]).astype(jnp.float32)
        totals = [parts[..., low:high] + part for (low, high), part in zip(edges, carried, strict=True)]
    away = [swap_cores(jnp.where(ahead, total[1], total[0]).astype(jnp.bfloat16)) for total in totals]
    ours = [jnp.where(ahead, total[0], total[1]) for total in totals]
    return jnp.concatenate(ours, axis=-1), jnp.concatenate(away, axis=-1)


def attention_kernel(decay_ref, ours_ref, our_sums_ref, theirs_ref, their_sums_ref, state_ref, gain_ref, mask_ref, out_ref):
    head = pl.program_id(0)
    rows = ours_ref.shape[0]
    mine = rows // STEPS
    squares = jnp.sum(our_sums_ref[...] + their_sums_ref[...].astype(jnp.float32), axis=-1, keepdims=True)
    parts = (ours_ref[...] + theirs_ref[...].astype(jnp.float32)) * lax.rsqrt(squares / D + EPS)
    scale = DH ** (-0.5)
    queries = parts[:, :DH] * scale
    keys = parts[:, DH : 2 * DH] * scale
    values = parts[:, 2 * DH :]
    rate = decay_ref[head]
    tiled = jnp.concatenate([queries] * mine, axis=1)
    row = lax.broadcasted_iota(jnp.int32, tiled.shape, 0) % mine
    column = lax.broadcasted_iota(jnp.int32, tiled.shape, 1) // DH
    left = jnp.where(row == column, tiled, 0.0)
    left_high = left.astype(jnp.bfloat16)
    left_low = (left - left_high.astype(jnp.float32)).astype(jnp.bfloat16)
    right = state_ref[...].reshape(mine * DH, DH)
    right_high = right.astype(jnp.bfloat16)
    right_low = (right - right_high.astype(jnp.float32)).astype(jnp.bfloat16)
    both = jnp.concatenate([left_high, left_low], axis=0)
    found = jnp.dot(both, right_high, preferred_element_type=jnp.float32)
    found = found + jnp.dot(both, right_low, preferred_element_type=jnp.float32)
    found = found[:rows] + found[rows:]
    power = rate
    for step in range(STEPS):
        here = slice(step * mine, (step + 1) * mine)
        total = power * found[here]
        power = power * rate
        factor = None
        for earlier in range(step, -1, -1):
            there = slice(earlier * mine, (earlier + 1) * mine)
            score = jnp.sum(queries[here] * keys[there], axis=-1, keepdims=True)
            if factor is not None:
                score = score * factor
            total = total + score * values[there]
            factor = rate if factor is None else factor * rate
        total = total * lax.rsqrt(jnp.mean(total * total, axis=-1, keepdims=True) + EPS)
        spiked = total * gain_ref[...] * mask_ref[step].astype(jnp.float32)
        out_ref[here, :] = spiked.astype(jnp.bfloat16)


def attention(decay, ours, theirs, state, head_gain, att_mask):
    rows, width = ours.shape
    mine, heads = state.shape[:2]
    last = width // LANES - 1
    return pl.pallas_call(
        attention_kernel,
        grid=(heads,),
        in_specs=[
            pl.BlockSpec(memory_space=pltpu.SMEM),
            pl.BlockSpec((rows, 3 * DH), lambda h: (0, h)),
            pl.BlockSpec((rows, LANES), lambda h: (0, last)),
            pl.BlockSpec((rows, 3 * DH), lambda h: (0, h)),
            pl.BlockSpec((rows, LANES), lambda h: (0, last)),
            pl.BlockSpec((mine, 1, DH, DH), lambda h: (0, h, 0, 0)),
            pl.BlockSpec((1, DH), lambda h: (0, h)),
            pl.BlockSpec((STEPS, mine, DH), lambda h: (0, 0, h)),
        ],
        out_specs=pl.BlockSpec((rows, DH), lambda h: (0, h)),
        out_shape=jax.ShapeDtypeStruct((rows, heads * DH), jnp.bfloat16),
        compiler_params=VMEM,
    )(decay, ours, ours, theirs, theirs, pltpu.with_memory_space_constraint(state, pltpu.HBM), head_gain[None, :], att_mask)


def mix_kernel(place_ref, partial_ref, inputs_ref, gain_ref, mixed_ref, hidden_ref):
    share = inputs_ref.shape[1]
    for step in range(STEPS):
        here = slice(step * share, (step + 1) * share)
        total = inputs_ref[step].astype(jnp.float32)
        for source in range(partial_ref.shape[0]):
            total = total + partial_ref[source, here, :].astype(jnp.float32)
        mixed_ref[here, :] = total
        hidden = (total * gain_ref[...]).astype(jnp.bfloat16)
        for target in range(hidden_ref.shape[0]):
            hidden_ref[target, here, :] = hidden


def mix(place, partial, inputs, gain):
    blocks, each, features = partial.shape
    whole = pl.BlockSpec((blocks, each, features), lambda i, place: (0, 0, 0))
    return pl.pallas_call(
        mix_kernel,
        grid_spec=pltpu.PrefetchScalarGridSpec(
            num_scalar_prefetch=1,
            grid=(1,),
            in_specs=[
                whole,
                pl.BlockSpec((STEPS, each // STEPS, features), lambda i, place: (0, place[3], 0)),
                pl.BlockSpec((1, features), lambda i, place: (0, 0)),
            ],
            out_specs=[pl.BlockSpec((each, features), lambda i, place: (0, 0)), whole],
        ),
        out_shape=[
            jax.ShapeDtypeStruct((each, features), jnp.float32),
            jax.ShapeDtypeStruct(partial.shape, jnp.bfloat16),
        ],
        compiler_params=VMEM,
    )(place, partial, pltpu.with_memory_space_constraint(inputs, pltpu.HBM), gain[None, :])


def gathered_product(value, weight):
    zs = lax.axis_size("z")
    half = zs // 2
    z, core = lax.axis_index("z"), lax.axis_index("core")
    towards = jnp.where(core == 0, -1, 1)
    rows, width = value.shape[0], weight.shape[1]
    out = jnp.zeros((zs, 2, rows, width), jnp.bfloat16)

    def multiply(blocks):
        return jnp.dot(blocks.reshape(-1, blocks.shape[-1]), weight, preferred_element_type=jnp.float32).astype(
            jnp.bfloat16
        ).reshape(blocks.shape[:-1] + (width,))

    def put(out, blocks, chip):
        return lax.dynamic_update_slice(out, blocks[None], ((chip + zs) % zs, 0, 0, 0))

    sibling = swap_cores(value)
    low, high = jnp.where(core == 0, value, sibling), jnp.where(core == 0, sibling, value)
    moving = jnp.stack([low, high])
    edges = edges_of(value.shape[1], GATHER_CHAINS)
    moving = [moving[..., low:high] for low, high in edges]
    weights = [weight[low:high] for low, high in edges]

    def multiply(blocks):
        total = 0.0
        for block, part in zip(blocks, weights, strict=True):
            total = total + jnp.dot(block.reshape(-1, block.shape[-1]), part, preferred_element_type=jnp.float32)
        return total.astype(jnp.bfloat16).reshape(blocks[0].shape[:-1] + (width,))

    out = put(out, multiply(moving), z)
    for distance in range(1, half):
        moving = [pass_on(part) for part in moving]
        other = [swap_cores(part) for part in moving]
        done = multiply([jnp.stack([a, b]) for a, b in zip(moving, other, strict=True)])
        out = put(out, done[0], z + towards * distance)
        out = put(out, done[1], z - towards * distance)
    return put(out, multiply([pass_on(part) for part in moving]), z + half)


def on_device(
    inputs,
    in_gain,
    qkv_weight,
    decay,
    state,
    head_gain,
    out_weight,
    mid_gain,
    up_weight,
    down_weight,
    att_mask,
    ffn_mask,
):
    blocks = lax.axis_size("core") * lax.axis_size("z")
    share = inputs.shape[1] // blocks
    features = inputs.shape[2]
    each = STEPS * share
    zs = lax.axis_size("z")
    z, core = lax.axis_index("z"), lax.axis_index("core")
    ahead = core == 0
    theirs_from = jnp.where(ahead, z + zs // 2, z + 1) % zs
    mine_from = jnp.where(ahead, z, z + zs // 2) % zs
    place = jnp.stack([theirs_from, mine_from, z * 2 + core, lax.axis_index(TENSOR)]).astype(jnp.int32)
    ours, theirs = sum_to_owner(inputs, in_gain, qkv_weight, place, ahead, True)
    spiked = attention(decay, ours, theirs, state, head_gain, att_mask)

    everyone = lax.all_gather(spiked, BATCH, axis=0, tiled=True)
    partial = jnp.dot(everyone, out_weight, preferred_element_type=jnp.float32).astype(jnp.bfloat16)
    partial = partial.reshape(blocks, each, features)
    partial = lax.all_to_all(partial, TENSOR, 0, 0, tiled=True)
    mixed, hidden = mix(place, partial, inputs, mid_gain)
    hidden = lax.all_to_all(hidden, TENSOR, 0, 0, tiled=True)
    ours, theirs = sum_to_owner(hidden, mid_gain, up_weight, place, ahead, False)
    total = ours + theirs.astype(jnp.float32)
    units = up_weight.shape[1]
    inverse = lax.rsqrt(jnp.sum(total[:, units:], axis=-1, keepdims=True) / D + EPS)
    gate = total[:, :units] * inverse
    fired = ffn_mask.reshape(each, units) * (gate / (1.0 + jnp.exp(-gate)))

    partial = gathered_product(fired.astype(jnp.bfloat16), down_weight)
    partial = lax.all_to_all(partial.reshape(blocks, each, features), TENSOR, 0, 0, tiled=True)
    final = mixed + jnp.sum(partial.astype(jnp.float32), axis=0)
    return final.astype(jnp.bfloat16).reshape(STEPS, share, features)


def solution(mesh):
    devices = mesh.devices.reshape(8, 2, 4, 4)
    inner = Mesh(devices, ("z", "core", "y", "x"))
    return jax.shard_map(
        on_device,
        mesh=inner,
        in_specs=(
            P(None, None, BATCH),
            P(BATCH),
            P(BATCH, TENSOR),
            P(TENSOR),
            P(BATCH, TENSOR, None, None),
            P(TENSOR),
            P(TENSOR, BATCH),
            P(BATCH),
            P(BATCH, TENSOR),
            P(TENSOR, BATCH),
            P(None, BATCH, TENSOR),
            P(None, BATCH, TENSOR),
        ),
        out_specs=P(None, TENSOR, BATCH),
        check_vma=False,
    )
```

```python
import functools

import jax
import jax.numpy as jnp
from jax import lax
from jax.experimental import pallas as pl
from jax.experimental.pallas import tpu as pltpu
from jax.sharding import Mesh
from jax.sharding import PartitionSpec as P

D = 8192
STEPS = 3
DH = 128
EPS = 1e-06
LANES = 128
CHAINS = 2
GATHER_CHAINS = 2
BATCH = ("z", "core")
TENSOR = ("y", "x")
VMEM = pltpu.CompilerParams(vmem_limit_bytes=14 * 1024 * 1024)


def edges_of(width, count):
    tiles = width // LANES
    cuts = [LANES * (tiles * i // count) for i in range(count + 1)]
    return list(zip(cuts[:-1], cuts[1:], strict=True))


def swap_cores(value):
    return lax.ppermute(value, "core", [(0, 1), (1, 0)])


def pass_on(value):
    zs = lax.axis_size("z")
    pairs = []
    for z in range(zs):
        pairs.append((2 * z, 2 * ((z + 1) % zs)))
        pairs.append((2 * z + 1, 2 * ((z - 1) % zs) + 1))
    return lax.ppermute(value, BATCH, pairs)


def pieces_of(sums, source):
    high = lax.reduce_precision(sums, 8, 7)
    middle = lax.reduce_precision(sums - high, 8, 7)
    low = sums - high - middle
    lane = lax.broadcasted_iota(jnp.int32, (sums.shape[0], LANES), 1) - 3 * source
    return jnp.where(lane == 0, high, jnp.where(lane == 1, middle, jnp.where(lane == 2, low, 0.0)))


def product_kernel(chips, first, which, place_ref, rows_ref, gain_ref, weight_ref, out_ref, picked_ref):
    width = weight_ref.shape[1]
    share = picked_ref.shape[0] // (2 * STEPS * chips)
    zs = rows_ref.shape[1] // (2 * share) if first else rows_ref.shape[0] // 2
    start, source = place_ref[which], place_ref[2]
    gain = gain_ref[...] if first else 1.0 / gain_ref[...]
    for c in range(chips):
        chip = start + c
        chip = jnp.where(chip >= zs, chip - zs, chip)
        for core in range(2):
            for step in range(STEPS):
                at = ((c * 2 + core) * STEPS + step) * share
                if first:
                    from_row = pl.multiple_of(chip * (2 * share) + core * share, share)
                    values = rows_ref[step, pl.ds(from_row, share), :].astype(jnp.float32)
                    picked_ref[at : at + share, :] = (values * gain).astype(jnp.bfloat16)
                else:
                    block = rows_ref[chip * 2 + core, step * share : (step + 1) * share, :]
                    picked_ref[at : at + share, :] = block
                    values = block.astype(jnp.float32) * gain
                squares = jnp.sum(values * values, axis=-1, keepdims=True)
                out_ref[at : at + share, width:] = pieces_of(squares, source).astype(out_ref.dtype)
    chunk = width // 2
    for at in range(0, width, chunk):
        out_ref[:, at : at + chunk] = jnp.dot(
            picked_ref[...], weight_ref[:, at : at + chunk], preferred_element_type=jnp.float32
        ).astype(out_ref.dtype)


def product(rows, gain, weight, chips, which, place, first):
    share = (rows.shape[1] // 16) if first else rows.shape[1] // STEPS
    count = chips * 2 * STEPS * share
    depth, width = weight.shape
    if first:
        rows = pltpu.with_memory_space_constraint(rows, pltpu.HBM)
        weight = pltpu.with_memory_space_constraint(weight, pltpu.HBM)
    out = pl.pallas_call(
        functools.partial(product_kernel, chips, first, which),
        in_specs=[pl.BlockSpec(memory_space=pltpu.SMEM)] + [pl.BlockSpec(memory_space=pltpu.VMEM)] * 3,
        out_specs=pl.BlockSpec(memory_space=pltpu.VMEM),
        out_shape=jax.ShapeDtypeStruct((count, width + LANES), jnp.bfloat16),
        scratch_shapes=[pltpu.VMEM((count, depth), jnp.bfloat16)],
        compiler_params=VMEM,
    )(place, rows, gain[None, :], weight)
    return out.reshape(chips, 2, STEPS * share, width + LANES)


def sum_to_owner(rows, gain, weight, place, ahead, first):
    half = lax.axis_size("z") // 2
    theirs = product(rows, gain, weight, half, 0, place, first)
    got = swap_cores(theirs)
    mine = product(rows, gain, weight, half + 1, 1, place, first)

    def at(distance):
        own = jnp.where(ahead, mine[distance], mine[half - distance]).astype(jnp.float32)
        other = jnp.where(ahead, got[distance - 1], got[half - distance]).astype(jnp.float32)
        return own + other

    width = mine.shape[-1]
    edges = edges_of(width, CHAINS)
    which = (lax.broadcasted_iota(jnp.int32, (2, 1, 1), 0) == 0) == ahead
    farthest = at(half)
    carried = jnp.where(ahead, farthest[0], farthest[1]).astype(jnp.bfloat16)
    carried = [pass_on(carried[:, low:high]) for low, high in edges]
    parts = at(half - 1)
    totals = [
        parts[..., low:high] + jnp.where(which, part.astype(jnp.float32)[None], 0.0)
        for (low, high), part in zip(edges, carried, strict=True)
    ]
    for distance in range(half - 2, -1, -1):
        carried = [pass_on(total.astype(jnp.bfloat16)).astype(jnp.float32) for total in totals]
        parts = at(distance) if distance > 0 else jnp.where(ahead, mine[0], mine[half]).astype(jnp.float32)
        totals = [parts[..., low:high] + part for (low, high), part in zip(edges, carried, strict=True)]
    away = [swap_cores(jnp.where(ahead, total[1], total[0]).astype(jnp.bfloat16)) for total in totals]
    ours = [jnp.where(ahead, total[0], total[1]) for total in totals]
    return jnp.concatenate(ours, axis=-1), jnp.concatenate(away, axis=-1)


def attention_kernel(decay_ref, ours_ref, our_sums_ref, theirs_ref, their_sums_ref, state_ref, gain_ref, mask_ref, out_ref):
    head = pl.program_id(0)
    rows = ours_ref.shape[0]
    mine = rows // STEPS
    squares = jnp.sum(our_sums_ref[...] + their_sums_ref[...].astype(jnp.float32), axis=-1, keepdims=True)
    parts = (ours_ref[...] + theirs_ref[...].astype(jnp.float32)) * lax.rsqrt(squares / D + EPS)
    scale = DH ** (-0.5)
    queries = parts[:, :DH] * scale
    keys = parts[:, DH : 2 * DH] * scale
    values = parts[:, 2 * DH :]
    rate = decay_ref[head]
    tiled = jnp.concatenate([queries] * mine, axis=1)
    row = lax.broadcasted_iota(jnp.int32, tiled.shape, 0) % mine
    column = lax.broadcasted_iota(jnp.int32, tiled.shape, 1) // DH
    left = jnp.where(row == column, tiled, 0.0)
    left_high = left.astype(jnp.bfloat16)
    left_low = (left - left_high.astype(jnp.float32)).astype(jnp.bfloat16)
    right = state_ref[...].reshape(mine * DH, DH)
    right_high = right.astype(jnp.bfloat16)
    right_low = (right - right_high.astype(jnp.float32)).astype(jnp.bfloat16)
    both = jnp.concatenate([left_high, left_low], axis=0)
    found = jnp.dot(both, right_high, preferred_element_type=jnp.float32)
    found = found + jnp.dot(both, right_low, preferred_element_type=jnp.float32)
    found = found[:rows] + found[rows:]
    power = rate
    for step in range(STEPS):
        here = slice(step * mine, (step + 1) * mine)
        total = power * found[here]
        power = power * rate
        factor = None
        for earlier in range(step, -1, -1):
            there = slice(earlier * mine, (earlier + 1) * mine)
            score = jnp.sum(queries[here] * keys[there], axis=-1, keepdims=True)
            if factor is not None:
                score = score * factor
            total = total + score * values[there]
            factor = rate if factor is None else factor * rate
        total = total * lax.rsqrt(jnp.mean(total * total, axis=-1, keepdims=True) + EPS)
        spiked = total * gain_ref[...] * mask_ref[step].astype(jnp.float32)
        out_ref[here, :] = spiked.astype(jnp.bfloat16)


def attention(decay, ours, theirs, state, head_gain, att_mask):
    rows, width = ours.shape
    mine, heads = state.shape[:2]
    last = width // LANES - 1
    return pl.pallas_call(
        attention_kernel,
        grid=(heads,),
        in_specs=[
            pl.BlockSpec(memory_space=pltpu.SMEM),
            pl.BlockSpec((rows, 3 * DH), lambda h: (0, h)),
            pl.BlockSpec((rows, LANES), lambda h: (0, last)),
            pl.BlockSpec((rows, 3 * DH), lambda h: (0, h)),
            pl.BlockSpec((rows, LANES), lambda h: (0, last)),
            pl.BlockSpec((mine, 1, DH, DH), lambda h: (0, h, 0, 0)),
            pl.BlockSpec((1, DH), lambda h: (0, h)),
            pl.BlockSpec((STEPS, mine, DH), lambda h: (0, 0, h)),
        ],
        out_specs=pl.BlockSpec((rows, DH), lambda h: (0, h)),
        out_shape=jax.ShapeDtypeStruct((rows, heads * DH), jnp.bfloat16),
        compiler_params=VMEM,
    )(decay, ours, ours, theirs, theirs, pltpu.with_memory_space_constraint(state, pltpu.HBM), head_gain[None, :], att_mask)


def mix_kernel(place_ref, partial_ref, inputs_ref, gain_ref, mixed_ref, hidden_ref):
    share = inputs_ref.shape[1]
    for step in range(STEPS):
        here = slice(step * share, (step + 1) * share)
        total = inputs_ref[step].astype(jnp.float32)
        for source in range(partial_ref.shape[0]):
            total = total + partial_ref[source, here, :].astype(jnp.float32)
        mixed_ref[here, :] = total
        hidden = (total * gain_ref[...]).astype(jnp.bfloat16)
        for target in range(hidden_ref.shape[0]):
            hidden_ref[target, here, :] = hidden


def mix(place, partial, inputs, gain):
    blocks, each, features = partial.shape
    whole = pl.BlockSpec((blocks, each, features), lambda i, place: (0, 0, 0))
    return pl.pallas_call(
        mix_kernel,
        grid_spec=pltpu.PrefetchScalarGridSpec(
            num_scalar_prefetch=1,
            grid=(1,),
            in_specs=[
                whole,
                pl.BlockSpec((STEPS, each // STEPS, features), lambda i, place: (0, place[3], 0)),
                pl.BlockSpec((1, features), lambda i, place: (0, 0)),
            ],
            out_specs=[pl.BlockSpec((each, features), lambda i, place: (0, 0)), whole],
        ),
        out_shape=[
            jax.ShapeDtypeStruct((each, features), jnp.float32),
            jax.ShapeDtypeStruct(partial.shape, jnp.bfloat16),
        ],
        compiler_params=VMEM,
    )(place, partial, pltpu.with_memory_space_constraint(inputs, pltpu.HBM), gain[None, :])


def gathered_product(value, weight):
    zs = lax.axis_size("z")
    half = zs // 2
    z, core = lax.axis_index("z"), lax.axis_index("core")
    towards = jnp.where(core == 0, -1, 1)
    rows, width = value.shape[0], weight.shape[1]
    out = jnp.zeros((zs, 2, rows, width), jnp.bfloat16)

    def multiply(blocks):
        return jnp.dot(blocks.reshape(-1, blocks.shape[-1]), weight, preferred_element_type=jnp.float32).astype(
            jnp.bfloat16
        ).reshape(blocks.shape[:-1] + (width,))

    def put(out, blocks, chip):
        return lax.dynamic_update_slice(out, blocks[None], ((chip + zs) % zs, 0, 0, 0))

    sibling = swap_cores(value)
    low, high = jnp.where(core == 0, value, sibling), jnp.where(core == 0, sibling, value)
    moving = jnp.stack([low, high])
    edges = edges_of(value.shape[1], GATHER_CHAINS)
    moving = [moving[..., low:high] for low, high in edges]
    weights = [weight[low:high] for low, high in edges]

    def multiply(blocks):
        total = 0.0
        for block, part in zip(blocks, weights, strict=True):
            total = total + jnp.dot(block.reshape(-1, block.shape[-1]), part, preferred_element_type=jnp.float32)
        return total.astype(jnp.bfloat16).reshape(blocks[0].shape[:-1] + (width,))

    out = put(out, multiply(moving), z)
    for distance in range(1, half):
        moving = [pass_on(part) for part in moving]
        other = [swap_cores(part) for part in moving]
        done = multiply([jnp.stack([a, b]) for a, b in zip(moving, other, strict=True)])
        out = put(out, done[0], z + towards * distance)
        out = put(out, done[1], z - towards * distance)
    return put(out, multiply([pass_on(part) for part in moving]), z + half)


def on_device(
    inputs,
    in_gain,
    qkv_weight,
    decay,
    state,
    head_gain,
    out_weight,
    mid_gain,
    up_weight,
    down_weight,
    att_mask,
    ffn_mask,
):
    blocks = lax.axis_size("core") * lax.axis_size("z")
    share = inputs.shape[1] // blocks
    features = inputs.shape[2]
    each = STEPS * share
    zs = lax.axis_size("z")
    z, core = lax.axis_index("z"), lax.axis_index("core")
    ahead = core == 0
    theirs_from = jnp.where(ahead, z + zs // 2, z + 1) % zs
    mine_from = jnp.where(ahead, z, z + zs // 2) % zs
    place = jnp.stack([theirs_from, mine_from, z * 2 + core, lax.axis_index(TENSOR)]).astype(jnp.int32)
    ours, theirs = sum_to_owner(inputs, in_gain, qkv_weight, place, ahead, True)
    spiked = attention(decay, ours, theirs, state, head_gain, att_mask)

    everyone = lax.all_gather(spiked, BATCH, axis=0, tiled=True)
    partial = jnp.dot(everyone, out_weight, preferred_element_type=jnp.float32).astype(jnp.bfloat16)
    partial = partial.reshape(blocks, each, features)
    partial = lax.all_to_all(partial, TENSOR, 0, 0, tiled=True)
    mixed, hidden = mix(place, partial, inputs, mid_gain)
    hidden = lax.all_to_all(hidden, TENSOR, 0, 0, tiled=True)
    ours, theirs = sum_to_owner(hidden, mid_gain, up_weight, place, ahead, False)
    total = ours + theirs.astype(jnp.float32)
    units = up_weight.shape[1]
    inverse = lax.rsqrt(jnp.sum(total[:, units:], axis=-1, keepdims=True) / D + EPS)
    gate = total[:, :units] * inverse
    fired = ffn_mask.reshape(each, units) * (gate / (1.0 + jnp.exp(-gate)))

    partial = gathered_product(fired.astype(jnp.bfloat16), down_weight)
    partial = lax.all_to_all(partial.reshape(blocks, each, features), TENSOR, 0, 0, tiled=True)
    final = mixed + jnp.sum(partial.astype(jnp.float32), axis=0)
    return final.astype(jnp.bfloat16).reshape(STEPS, share, features)


def solution(mesh):
    devices = mesh.devices.reshape(8, 2, 4, 4)
    inner = Mesh(devices, ("z", "core", "y", "x"))
    return jax.shard_map(
        on_device,
        mesh=inner,
        in_specs=(
            P(None, None, BATCH),
            P(BATCH),
            P(BATCH, TENSOR),
            P(TENSOR),
            P(BATCH, TENSOR, None, None),
            P(TENSOR),
            P(TENSOR, BATCH),
            P(BATCH),
            P(BATCH, TENSOR),
            P(TENSOR, BATCH),
            P(None, BATCH, TENSOR),
            P(None, BATCH, TENSOR),
        ),
        out_specs=P(None, TENSOR, BATCH),
        check_vma=False,
    )
```
